128 devices in a mesh: dp: 8 (over x, core), expert: 16 (over y, z).
Axes of the slice: x: 4, y: 4, z: 4, core: 2. Of those that a mesh axis runs over, the one named last changes fastest.
Arguments:
- out_grad: bfloat16 [32768, 2048], P(('dp', 'expert')), may hold values from -6 to 6
- expert_ids: int32 [32768, 2], P(('dp', 'expert')), may hold values from 0 to 15, all different within a row; in each aligned block of 256 rows (0 to 255, 256 to 511, ...) at most 64 rows name the same one
- gates: float32 [32768, 2], P(('dp', 'expert')), may hold values from 0.1 to 0.9
- hidden_slots: bfloat16 [8, 16, 16, 64, 3200], P('dp', 'expert'), may hold values from -6 to 6
- weights: bfloat16 [16, 3200, 2048], P('expert', 'dp'), may hold values from -0.109375 to 0.109375
- mom_codes: bfloat16 [16, 3200, 2048], P('expert', 'dp'), may hold values from -1 to 1
- mom_scales: float32 [16, 3200], P('expert', 'dp'), may hold values from 0.02 to 0.5
Outputs:
- hidden_grad: bfloat16 [32768, 2, 3200], P(('dp', 'expert'))
- update_dir: bfloat16 [16, 3200, 2048], P('expert', 'dp')
- new_codes: bfloat16 [16, 3200, 2048], P('expert', 'dp')
- new_scales: float32 [16, 3200], P('expert', 'dp')
The draws below stay inside these ranges and needn't reach their ends.
Inputs may be any that keep to these rules, and one draw needn't show every extreme that they name: `expert_ids`: in each aligned block of 256 tokens (the tokens of one device) no expert is named by more than 64 tokens; a token names two different experts.
All inputs are finite; a program needn't handle non-finite values. Where the reference program divides by a largest or mean magnitude, that divisor is 1e-20 or more.
Results may differ from the reference program's by a relative error of at most 0.012.
Values may be sent and summed in bfloat16 or wider, within the bound.
A program may use at most 128 MiB of HBM per device.

```python
import math
import jax
import jax.numpy as jnp
import numpy as np
from jax import lax

D = 2048
FF = 3200
TOK_DEV = 256
CAP = 64
EXPERTS = 16
TOKENS = 32768
N_DP = 8
N_EXPERT = 16


def levels(key, extent, cuts, smallest, largest):
    def one(position, shards_of):
        steps = jax.random.uniform(jax.random.fold_in(jax.random.fold_in(key, 6), position), (shards_of,), jnp.float32, smallest / len(cuts), largest / len(cuts))
        return jnp.repeat(jnp.exp(steps), extent[position] // shards_of).reshape((-1,) + (1,) * (len(extent) - position - 1))

    level = one(*cuts[0])
    for cut in cuts[1:]:
        level = level * one(*cut)
    return level


def shared_out(rng, own, number, rows, count, top, reach, lean):
    sequence = jax.random.permutation(rng, count)
    heavy_load, usual = load_shares(count, rows * top, reach, lean, True), load_shares(count, rows * top, reach, lean, False)
    places = jnp.arange(count)

    def named(tallies, offset_by):
        used = int((tallies > 0).sum())
        fixed = max(1, used // 4)
        shifted = fixed + (places - fixed + offset_by * (used - fixed)) % max(1, count - fixed)
        return jnp.zeros((count,), jnp.int32).at[sequence[jnp.where(places < fixed, places, shifted)]].set(jnp.asarray(tallies, jnp.int32))

    tallies = jnp.where(number % 4 == 0, named(heavy_load, number // 4), named(usual, number - number // 4 - 1))
    mixed = jax.random.permutation(jax.random.fold_in(own, 3), count)
    giver, sink = mixed[0:count // 2 * 2:2], mixed[1:count // 2 * 2:2]
    room = jnp.minimum(tallies[giver] - 1, reach - tallies[sink]) // 2
    room = jnp.where((giver == sequence[0]) | (sink == sequence[0]) | (tallies[sink] == 0), 0, jnp.maximum(room, 0))
    shifted = jax.random.randint(jax.random.fold_in(own, 4), (count // 2,), 0, 1 << 20) % (room + 1)
    tallies = tallies.at[giver].add(-shifted).at[sink].add(shifted)
    members = jnp.searchsorted(jnp.cumsum(tallies), jnp.arange(rows * top), side="right").astype(jnp.int32)
    listing = members.reshape(top, rows).T
    listing = listing[jax.random.permutation(jax.random.fold_in(own, 1), rows)]
    offset_by = jax.random.randint(jax.random.fold_in(own, 2), (rows, 1), 0, top)
    return jnp.take_along_axis(listing, (jnp.arange(top)[None, :] + offset_by) % top, axis=1)


def load_shares(count, total, limit, lean, full):
    portions = [(1 << 20) // math.isqrt(grade ** lean) + 1 for grade in range(1, count + 1)]
    largest = limit if full else min(limit, max(-(-total // count), total * portions[0] // sum(portions)))
    least = 1 if total - largest >= count - 1 else 0
    counts, rest = [largest] + [least] * (count - 1), total - largest - least * (count - 1)
    while rest > 0:
        candidates = [i for i in range(1, count) if counts[i] < largest] or [i for i in range(1, count) if counts[i] < limit]
        mass, remaining = sum([portions[i] for i in candidates]), rest
        for i in candidates:
            addition = min(limit - counts[i], max(1, remaining * portions[i] // mass), rest)
            counts[i] = counts[i] + addition
            rest = rest - addition
    return np.array(counts)


def centred(stream_key, dims, scale, limit, pieces=(), kind=jnp.bfloat16):
    loudness = levels(stream_key, dims, pieces, -0.22, 0.18) if pieces else 1.0
    array = jax.random.normal(stream_key, dims, jnp.float32) * scale * loudness
    return jnp.minimum(jnp.maximum(array, -limit), limit).astype(kind)


def setup_inputs(seed: int = 0) -> dict:
    keys = jax.random.split(jax.random.key(seed), 8)
    out_grad = centred(keys[0], (TOKENS, D), 1.0, 6.0, ((0, 128),))
    expert_ids_keys = jax.random.split(jax.random.fold_in(keys[1], 1), TOKENS // TOK_DEV)
    expert_ids_turns = jax.random.permutation(jax.random.fold_in(keys[1], 3), TOKENS // TOK_DEV)
    expert_ids = jax.vmap(lambda own, number: shared_out(jax.random.fold_in(keys[1], 2), own, number, TOK_DEV, EXPERTS, 2, CAP, 1))(expert_ids_keys, expert_ids_turns).reshape((TOKENS, 2))
    gates = jnp.clip(0.1 + 0.79999997 * jax.random.uniform(keys[2], (TOKENS, 2), jnp.float32) ** levels(keys[2], (TOKENS, 2), ((0, 128),), -0.2, 0.2), 0.1, 0.9)
    hidden_slots = centred(keys[3], (N_DP, EXPERTS, N_EXPERT, CAP, FF), 1.0, 6.0, ((0, 8), (1, 16)))
    weights = centred(keys[4], (EXPERTS, FF, D), FF ** -0.5, 0.109375, ((0, 16), (1, 8)))
    mom_codes = jnp.clip(jax.random.uniform(keys[5], (EXPERTS, FF, D), jnp.float32, -1.0, 1.0) * levels(keys[5], (EXPERTS, FF, D), ((0, 16), (1, 8)), -0.4, 0.0), -1.0, 1.0).astype(jnp.bfloat16)
    mom_scales = jnp.clip(jnp.exp(math.log(0.5) - 3.218876 * jax.random.uniform(keys[6], (EXPERTS, FF), jnp.float32) ** levels(keys[6], (EXPERTS, FF), ((0, 16), (1, 8)), -0.2, 0.2)), 0.02, 0.5)
    return {"out_grad": out_grad, "expert_ids": expert_ids, "gates": gates, "hidden_slots": hidden_slots, "weights": weights, "mom_codes": mom_codes, "mom_scales": mom_scales}


beta_one = 0.9
beta_two = 0.99
epsilon = 1e-06

def reference(out_grad, expert_ids, gates, hidden_slots, weights, mom_codes, mom_scales):
    groups = N_DP
    sources = N_EXPERT
    row_count = TOK_DEV * 2
    scaled_rows = (gates[:, :, None] * out_grad[:, None, :].astype(jnp.float32)).astype(jnp.bfloat16)
    scaled_rows = scaled_rows.reshape(groups, sources, row_count, D)
    route_ids = expert_ids.reshape(groups, sources, row_count).astype(jnp.int32)
    onehot = (route_ids[..., None] == jnp.arange(EXPERTS, dtype=jnp.int32)).astype(jnp.int32)
    slot_pos = lax.optimization_barrier(jnp.sum((jnp.cumsum(onehot, axis=2) - 1) * onehot, axis=-1)).astype(jnp.int32)
    group_idx = jnp.arange(groups, dtype=jnp.int32)[:, None, None]
    source_idx = jnp.arange(sources, dtype=jnp.int32)[None, :, None]
    slot_grads = jnp.zeros((groups, EXPERTS, sources, CAP, D), jnp.bfloat16)
    slot_grads = slot_grads.at[group_idx, route_ids, source_idx, slot_pos].set(scaled_rows)

    def per_expert(index):
        rows_e = lax.dynamic_index_in_dim(slot_grads, index, 1, keepdims=False)
        hid_e = lax.dynamic_index_in_dim(hidden_slots, index, 1, keepdims=False)
        weight_e = lax.dynamic_index_in_dim(weights, index, 0, keepdims=False)

        def one_group(pair):
            hid_g, rows_g = pair
            return jnp.dot(hid_g.reshape(-1, FF).T, rows_g.reshape(-1, D), preferred_element_type=jnp.float32).astype(jnp.bfloat16)
        partials = lax.map(one_group, (hid_e, rows_e))
        grad_sum = lax.optimization_barrier(jnp.sum(partials.astype(jnp.float32), axis=0))
        slot_hidden = jnp.dot(rows_e.reshape(-1, D), weight_e.T, preferred_element_type=jnp.float32).astype(jnp.bfloat16)
        return (grad_sum, slot_hidden.reshape(groups, sources, CAP, FF))
    grad_sums, slot_hidden = lax.map(per_expert, jnp.arange(EXPERTS, dtype=jnp.int32))
    slot_hidden = jnp.moveaxis(slot_hidden, 0, 1)
    hidden_grad = slot_hidden[group_idx, route_ids, source_idx, slot_pos]
    hidden_grad = hidden_grad.reshape(TOKENS, 2, FF)
    gradient = math.sqrt(EXPERTS / (2.0 * TOKENS)) * grad_sums
    momentum = mom_codes.astype(jnp.float32) * mom_scales[:, :, None]
    blended = beta_one * momentum + (1.0 - beta_one) * gradient
    root_mean = jnp.sqrt(lax.optimization_barrier(jnp.mean(blended * blended, axis=-1, keepdims=True)) + epsilon)
    update_dir = jnp.tanh(blended / root_mean).astype(jnp.bfloat16)
    advanced = beta_two * momentum + (1.0 - beta_two) * gradient
    new_scales = lax.optimization_barrier(jnp.max(jnp.abs(advanced), axis=-1)) + epsilon
    new_codes = (advanced / new_scales[:, :, None]).astype(jnp.bfloat16)
    return (hidden_grad, update_dir, new_codes, new_scales)
```

```python
import functools
import math

import jax
import jax.numpy as jnp
from jax import lax
from jax.experimental import pallas as pl
from jax.experimental.pallas import tpu as pltpu
from jax.sharding import PartitionSpec as P

MESH = pl.DeviceIdType.MESH
bf16 = jnp.bfloat16
f32 = jnp.float32

beta_one = 0.9
beta_two = 0.99
epsilon = 1e-06

D = 2048
FF = 3200
TOK = 256
CAP = 64
HALF = 32
SHARD = 400
CUT = 208
NCH = 5
C = FF // NCH


def slot_keys(ids):
    tok = ids.shape[1]
    expert = lax.broadcasted_iota(jnp.int32, (16, tok), 0)
    c0 = expert == ids[0:1, :]
    c1 = expert == ids[1:2, :]
    cnt = jnp.where(c0 | c1, 1.0, 0.0).astype(bf16)
    before = jnp.where(
        lax.broadcasted_iota(jnp.int32, (tok, tok), 0) < lax.broadcasted_iota(jnp.int32, (tok, tok), 1), 1.0, 0.0
    ).astype(bf16)
    earlier = jnp.dot(cnt, before, preferred_element_type=f32)
    pos0 = jnp.sum(jnp.where(c0, earlier, 0.0), axis=0, keepdims=True).astype(jnp.int32)
    pos1 = jnp.sum(jnp.where(c1, earlier, 0.0), axis=0, keepdims=True).astype(jnp.int32)
    return ids[0:1, :] * CAP + pos0, ids[1:2, :] * CAP + pos1


def rows_of(start, count):
    return pl.ds(pl.multiple_of(start, 16), count)


def main_kernel(
    og, ids, gates, w, hid,
    ret, pieces, m1a, m1b, m2a, m2b,
    sb, rr, ww, ht, hbuf, pb, oo, sr, tt,
    ag_s, ag_r, loc, p1_s, p1_r, p2_s, p2_r, r1_s, r1_r, r2_s, r2_r, rl, sib_s, sib_r, x_s, x_r, hsem,
):
    dp = lax.axis_index("dp")
    ex = lax.axis_index("expert")
    x, c = dp // 2, dp % 2
    y, z = ex // 4, ex % 4

    def dev_x(d):
        return (((x + d) % 4) * 2 + c, ex)

    def dev_y(d):
        return (dp, ((y + d) % 4) * 4 + z)

    def dev_z(d):
        return (dp, y * 4 + (z + d) % 4)

    sibling = (x * 2 + 1 - c, ex)

    barrier = pltpu.get_barrier_semaphore()
    peers = [dev_y(1), dev_y(2), dev_y(3), dev_z(1), dev_z(2), dev_z(3), dev_x(1), dev_x(3), sibling]
    for peer in peers:
        pl.semaphore_signal(barrier, inc=1, device_id=peer, device_id_type=MESH)
    pl.semaphore_wait(barrier, len(peers))

    def remote(src, dst, s, r, device):
        return pltpu.make_async_remote_copy(
            src_ref=src, dst_ref=dst, send_sem=s, recv_sem=r, device_id=device, device_id_type=MESH
        )

    def shard_rows(xx, cc, lo, n):
        return rows_of(((xx % 4) * 2 + cc) * SHARD + lo, n)

    H0 = (0, CUT)
    H1 = (CUT, SHARD - CUT)

    def ag_copy(i, xx, cut, device, own):
        lo, n = cut
        there = ww.at[shard_rows(xx, c, lo, n)]
        src = w.at[pl.ds(lo, n)] if own else there
        return remote(src, there, ag_s.at[i], ag_r.at[i], device)

    ag = [
        ag_copy(0, x, H0, dev_x(1), True),
        ag_copy(1, x, H1, dev_x(1), True),
        ag_copy(2, x, H1, dev_x(3), True),
        ag_copy(3, x, H0, dev_x(3), True),
        ag_copy(4, x + 3, H0, dev_x(1), False),
        ag_copy(5, x + 1, H1, dev_x(3), False),
        ag_copy(6, x, (0, SHARD), sibling, True),
        ag_copy(7, x + 3, H0, sibling, False),
        ag_copy(8, x + 3, H1, sibling, False),
        ag_copy(9, x + 1, H1, sibling, False),
        ag_copy(10, x + 1, H0, sibling, False),
        ag_copy(11, x + 2, H0, sibling, False),
        ag_copy(12, x + 2, H1, sibling, False),
    ]
    w_own = pltpu.make_async_copy(w, ww.at[shard_rows(x, c, 0, SHARD)], loc.at[0])
    for i in (0, 2, 1, 3, 6):
        ag[i].start()
    w_own.start()

    def h_load(j):
        return pltpu.make_async_copy(hid.at[:, pl.ds(pl.multiple_of(j * C, 128), C)], hbuf.at[j % 2], hsem.at[j % 2])

    h_load(0).start()

    key0, key1 = slot_keys(ids[...])
    g0, g1 = gates[0:1, :], gates[1:2, :]

    def build(yy):
        slot = lax.broadcasted_iota(jnp.int32, (4 * CAP, TOK), 0) + yy * (4 * CAP)
        e0, e1 = slot == key0, slot == key1
        pick = jnp.where(e0 | e1, 1.0, 0.0).astype(bf16)
        gate = jnp.sum(jnp.where(e0, g0, 0.0) + jnp.where(e1, g1, 0.0), axis=1, keepdims=True)

        def cols(n, carry):
            at = pl.ds(pl.multiple_of(n * 512, 512), 512)
            rows = jnp.dot(pick, og[:, at], preferred_element_type=f32)
            sb[yy, :, :, at] = (rows * gate).astype(bf16).reshape(4, CAP, 512)
            return carry

        lax.fori_loop(0, 4, cols, 0)

    A = pl.ds(0, HALF)
    B = pl.ds(HALF, HALF)

    def p1a(d):
        return remote(sb.at[(y + d) % 4, :, A, :], m1a.at[y], p1_s.at[d - 1], p1_r.at[d - 1], dev_y(d))

    def p1b(d):
        return remote(sb.at[:, (z + d) % 4, B, :], m1b.at[z], p1_s.at[2 + d], p1_r.at[2 + d], dev_z(d))

    def p2a(j, d):
        sy = (y + 4 - j) % 4
        src = sb.at[y, (z + d) % 4, A, :] if j == 0 else m1a.at[sy, (z + d) % 4]
        i = j * 3 + d - 1
        return remote(src, rr.at[sy, z, A, :], p2_s.at[i], p2_r.at[i], dev_z(d))

    def p2b(j, d):
        sz = (z + 4 - j) % 4
        src = sb.at[(y + d) % 4, z, B, :] if j == 0 else m1b.at[sz, (y + d) % 4]
        i = 12 + j * 3 + d - 1
        return remote(src, rr.at[y, sz, B, :], p2_s.at[i], p2_r.at[i], dev_y(d))

    def p2a_own(j):
        sy = (y + 4 - j) % 4
        return pltpu.make_async_copy(m1a.at[sy, z], rr.at[sy, z, A, :], loc.at[1 + j])

    def p2b_own(j):
        sz = (z + 4 - j) % 4
        return pltpu.make_async_copy(m1b.at[sz, y], rr.at[y, sz, B, :], loc.at[4 + j])

    own_rows = pltpu.make_async_copy(sb.at[y, z], rr.at[y, z], loc.at[1])

    for d in (1, 3, 2):
        build((y + d) % 4)
        p1a(d).start()
    build(y)
    for d in (1, 3, 2):
        p1b(d).start()
    for d in (1, 3, 2):
        p2a(0, d).start()
        p2b(0, d).start()
    own_rows.start()

    def transpose_chunk(j):
        h_load(j).wait()
        if j + 1 < NCH:
            h_load(j + 1).start()

        def part(i, carry):
            at = pl.ds(pl.multiple_of(i * 128, 128), 128)
            ht[pl.ds(pl.multiple_of(j * C + i * 128, 128), 128), :] = hbuf[j % 2, :, at].T
            return carry

        lax.fori_loop(0, C // 128, part, 0)

    transpose_chunk(0)
    transpose_chunk(1)
    transpose_chunk(2)

    ag[0].wait_recv()
    ag[4].start()
    ag[7].start()
    ag[2].wait_recv()
    ag[5].start()
    ag[9].start()
    transpose_chunk(3)
    transpose_chunk(4)

    for j in (1, 3, 2):
        p1a(j).wait_recv()
        for d in (1, 3, 2):
            p2a(j, d).start()
        p2a_own(j).start()
        p1b(j).wait_recv()
        for d in (1, 3, 2):
            p2b(j, d).start()
        p2b_own(j).start()

    ag[1].wait_recv()
    ag[8].start()
    ag[3].wait_recv()
    ag[10].start()
    ag[4].wait_recv()
    ag[11].start()
    ag[5].wait_recv()
    ag[12].start()

    own_rows.wait()
    for j in (0, 1, 3, 2):
        for d in (1, 3, 2):
            p2a(j, d).wait_recv()
            p2b(j, d).wait_recv()
        if j:
            p2a_own(j).wait()
            p2b_own(j).wait()
    w_own.wait()
    for i in range(6, 13):
        ag[i].wait_recv()

    def product_a(j):
        wj = ww[pl.ds(j * C, C), :]

        def part(i, carry):
            rows = rr[i].reshape(4 * CAP, D)
            res = lax.dot_general(rows, wj, (((1,), (1,)), ((), ())), preferred_element_type=f32)
            oo[j, i] = res.astype(bf16).reshape(4, CAP, C)
            return carry

        lax.fori_loop(0, 4, part, 0)

    def product_b(j):
        hj = ht[pl.ds(j * C, C), :]

        def part(n, carry):
            at = pl.ds(pl.multiple_of(n * 256, 256), 256)
            rows = rr[:, :, :, at].reshape(16 * CAP, 256)
            pb[pl.ds(j * C, C), at] = jnp.dot(hj, rows, preferred_element_type=f32).astype(bf16)
            return carry

        lax.fori_loop(0, D // 256, part, 0)

    def r1a(j, d):
        return remote(oo.at[j, (y + d) % 4, :, A, :], m2a.at[j, y], r1_s.at[j, d - 1], r1_r.at[j, d - 1], dev_y(d))

    def r1b(j, d):
        return remote(oo.at[j, :, (z + d) % 4, B, :], m2b.at[j, z], r1_s.at[j, 2 + d], r1_r.at[j, 2 + d], dev_z(d))

    def r1a_own(j):
        return pltpu.make_async_copy(oo.at[j, y, :, A, :], m2a.at[j, y], rl.at[j, 0])

    def r1b_own(j):
        return pltpu.make_async_copy(oo.at[j, :, z, B, :], m2b.at[j, z], rl.at[j, 1])

    def r2a(j, d):
        return remote(
            m2a.at[j, :, (z + d) % 4], ret.at[j, :, z, A, :], r2_s.at[j, d - 1], r2_r.at[j, d - 1], dev_z(d)
        )

    def r2b(j, d):
        return remote(
            m2b.at[j, :, (y + d) % 4], ret.at[j, y, :, B, :], r2_s.at[j, 2 + d], r2_r.at[j, 2 + d], dev_y(d)
        )

    def r2a_own(j):
        return pltpu.make_async_copy(m2a.at[j, :, z], ret.at[j, :, z, A, :], rl.at[j, 2])

    def r2b_own(j):
        return pltpu.make_async_copy(m2b.at[j, :, y], ret.at[j, y, :, B, :], rl.at[j, 3])

    def send(j):
        for d in (1, 3, 2):
            r1a(j, d).start()
            r1b(j, d).start()
        r1a_own(j).start()
        r1b_own(j).start()

    def forward(j):
        r1a_own(j).wait()
        for d in (1, 3, 2):
            r1a(j, d).wait_recv()
        for d in (1, 3, 2):
            r2a(j, d).start()
        r2a_own(j).start()
        r1b_own(j).wait()
        for d in (1, 3, 2):
            r1b(j, d).wait_recv()
        for d in (1, 3, 2):
            r2b(j, d).start()
        r2b_own(j).start()

    hop = (2, 1, 3, 0)

    def to_sibling(k):
        return remote(pb.at[shard_rows(x + hop[k], 1 - c, 0, SHARD)], sr.at[k], sib_s.at[k], sib_r.at[k], sibling)

    def add_sibling(k):
        to_sibling(k).wait_recv()

        def part(i, carry):
            at = shard_rows(x + hop[k], c, i * 80, 80)
            mine = pb[at, :].astype(f32) + sr[k, pl.ds(pl.multiple_of(i * 80, 16), 80), :].astype(f32)
            pb[at, :] = mine.astype(bf16)
            return carry

        lax.fori_loop(0, SHARD // 80, part, 0)

    def far(i):
        lo, n = (H0, H1)[i]
        return remote(
            pb.at[shard_rows(x + 2, c, lo, n)], tt.at[pl.ds(lo, n)], x_s.at[i], x_r.at[i], dev_x((1, 3)[i])
        )

    def add_far(i):
        far(i).wait_recv()
        lo, n = (H0, H1)[i]

        def part(k, carry):
            at = shard_rows(x + (1, 3)[i], c, lo + k * 16, 16)
            mine = pb[at, :].astype(f32) + tt[pl.ds(pl.multiple_of(lo + k * 16, 16), 16), :].astype(f32)
            pb[at, :] = mine.astype(bf16)
            return carry

        lax.fori_loop(0, n // 16, part, 0)

    def near(i, h):
        lo, n = (H0, H1)[h]
        k = 2 + 2 * i + h
        return remote(
            pb.at[shard_rows(x + (1, 3)[i], c, lo, n)],
            pieces.at[1 + i, pl.ds(lo, n)],
            x_s.at[k],
            x_r.at[k],
            dev_x((1, 3)[i]),
        )

    own_piece = pltpu.make_async_copy(pb.at[shard_rows(x, c, 0, SHARD)], pieces.at[0], loc.at[8])

    product_a(0)
    send(0)
    product_a(1)
    send(1)
    product_b(0)
    product_b(1)
    forward(0)
    product_b(2)
    product_b(3)
    product_b(4)
    for k in range(4):
        to_sibling(k).start()
    product_a(2)
    send(2)
    forward(1)
    add_sibling(0)
    far(0).start()
    far(1).start()
    add_sibling(1)
    near(0, 1).start()
    add_sibling(2)
    near(1, 0).start()
    product_a(3)
    send(3)
    add_sibling(3)
    own_piece.start()
    product_a(4)
    send(4)
    forward(2)
    add_far(0)
    near(0, 0).start()
    add_far(1)
    near(1, 1).start()
    forward(3)
    forward(4)

    for i in range(13):
        ag[i].wait_send()
    for d in (1, 2, 3):
        p1a(d).wait_send()
        p1b(d).wait_send()
        for j in range(4):
            p2a(j, d).wait_send()
            p2b(j, d).wait_send()
    for k in range(4):
        to_sibling(k).wait_send()
    own_piece.wait()
    for i in range(2):
        far(i).wait_send()
        for h in range(2):
            near(i, h).wait()
    for j in range(NCH):
        r2a_own(j).wait()
        r2b_own(j).wait()
        for d in (1, 2, 3):
            r1a(j, d).wait_send()
            r1b(j, d).wait_send()
            r2a(j, d).wait()
            r2b(j, d).wait()


def main_call(og, ids, gates, w, hid):
    any_spec = pl.BlockSpec(memory_space=pl.ANY)
    vmem = pl.BlockSpec(memory_space=pltpu.VMEM)
    dma = pltpu.SemaphoreType.DMA
    s = jax.ShapeDtypeStruct
    return pl.pallas_call(
        main_kernel,
        out_shape=(
            s((NCH, 4, 4, CAP, C), bf16),
            s((3, SHARD, D), bf16),
            s((4, 4, HALF, D), bf16),
            s((4, 4, HALF, D), bf16),
            s((NCH, 4, 4, HALF, C), bf16),
            s((NCH, 4, 4, HALF, C), bf16),
        ),
        in_specs=[vmem, vmem, vmem, any_spec, any_spec],
        out_specs=[any_spec] * 6,
        scratch_shapes=[
            pltpu.VMEM((4, 4, CAP, D), bf16),
            pltpu.VMEM((4, 4, CAP, D), bf16),
            pltpu.VMEM((FF, D), bf16),
            pltpu.VMEM((FF, 16 * CAP), bf16),
            pltpu.VMEM((2, 16 * CAP, C), bf16),
            pltpu.VMEM((FF, D), bf16),
            pltpu.VMEM((NCH, 4, 4, CAP, C), bf16),
            pltpu.VMEM((4, SHARD, D), bf16),
            pltpu.VMEM((SHARD, D), bf16),
            dma((13,)), dma((13,)), dma((9,)),
            dma((6,)), dma((6,)), dma((24,)), dma((24,)),
            dma((NCH, 6)), dma((NCH, 6)), dma((NCH, 6)), dma((NCH, 6)), dma((NCH, 4)),
            dma((4,)), dma((4,)), dma((6,)), dma((6,)), dma((2,)),
        ],
        compiler_params=pltpu.CompilerParams(
            collective_id=0, has_side_effects=True, vmem_limit_bytes=63 * 2**20
        ),
        cost_estimate=pl.CostEstimate(flops=28 * 10**9, bytes_accessed=50 * 10**6, transcendentals=0),
        name="dispatch_products_return",
    )(og, ids, gates, w, hid)


def pick_kernel(ids, ret, out):
    key0, key1 = slot_keys(ids[...])
    slot = lax.broadcasted_iota(jnp.int32, (16 * CAP, TOK), 0)
    rows = ret[...].reshape(16 * CAP, C)
    for k, key in enumerate((key0, key1)):
        pick = jnp.where(slot == key, 1.0, 0.0).astype(bf16)
        got = lax.dot_general(pick, rows, (((0,), (0,)), ((), ())), preferred_element_type=f32)
        out[:, k, :] = got.astype(bf16)


def pick_call(ids, ret):
    return pl.pallas_call(
        pick_kernel,
        grid=(NCH,),
        out_shape=jax.ShapeDtypeStruct((TOK, 2, FF), bf16),
        in_specs=[
            pl.BlockSpec((2, TOK), lambda j: (0, 0)),
            pl.BlockSpec((None, 4, 4, CAP, C), lambda j: (j, 0, 0, 0, 0)),
        ],
        out_specs=pl.BlockSpec((TOK, 2, C), lambda j: (0, 0, j)),
        compiler_params=pltpu.CompilerParams(vmem_limit_bytes=48 * 2**20),
        name="pick_rows",
    )(ids, ret)


ROWS = 80


def step_kernel(factor, pieces, codes, scales, direction, new_codes, new_scales):
    i = pl.program_id(0)
    gradient = factor * (
        pieces[0].astype(f32) + pieces[1].astype(f32) + pieces[2].astype(f32)
    )
    here = lax.broadcasted_iota(jnp.int32, (ROWS, SHARD), 0) + i * ROWS == lax.broadcasted_iota(
        jnp.int32, (ROWS, SHARD), 1
    )
    scale = jnp.sum(jnp.where(here, scales[...], 0.0), axis=1, keepdims=True)
    momentum = codes[...].astype(f32) * scale
    blended = beta_one * momentum + (1.0 - beta_one) * gradient
    root = jnp.sqrt(jnp.mean(blended * blended, axis=-1, keepdims=True) + epsilon)
    direction[...] = jnp.tanh(blended / root).astype(bf16)
    advanced = beta_two * momentum + (1.0 - beta_two) * gradient
    largest = jnp.max(jnp.abs(advanced), axis=-1, keepdims=True) + epsilon
    new_codes[...] = (advanced / largest).astype(bf16)

    @pl.when(i == 0)
    def _():
        new_scales[...] = jnp.zeros_like(new_scales)

    new_scales[...] += jnp.sum(jnp.where(here, largest, 0.0), axis=0, keepdims=True)


def step_call(factor, pieces, codes, scales):
    block = pl.BlockSpec((ROWS, D), lambda i: (i, 0))
    line = pl.BlockSpec((1, SHARD), lambda i: (0, 0))
    return pl.pallas_call(
        functools.partial(step_kernel, factor),
        grid=(SHARD // ROWS,),
        out_shape=(
            jax.ShapeDtypeStruct((SHARD, D), bf16),
            jax.ShapeDtypeStruct((SHARD, D), bf16),
            jax.ShapeDtypeStruct((1, SHARD), f32),
        ),
        in_specs=[pl.BlockSpec((3, ROWS, D), lambda i: (0, i, 0)), block, line],
        out_specs=(block, block, line),
        compiler_params=pltpu.CompilerParams(vmem_limit_bytes=48 * 2**20),
        name="optimizer_step",
    )(pieces, codes, scales)


def local(out_grad, expert_ids, gates, hidden_slots, weights, mom_codes, mom_scales):
    experts = lax.axis_size("expert")
    groups = lax.axis_size("dp")
    tokens_all = out_grad.shape[0] * groups * experts
    ids = expert_ids.T
    ret, pieces, _, _, _, _ = main_call(
        out_grad, ids, gates.T, weights[0], hidden_slots.reshape(16 * CAP, FF)
    )
    hidden_grad = pick_call(ids, ret)
    factor = math.sqrt(experts / (2.0 * tokens_all))
    direction, new_codes, new_scales = step_call(factor, pieces, mom_codes[0], mom_scales)
    return (hidden_grad, direction[None], new_codes[None], new_scales)


def solution(mesh):
    in_specs = (
        P(("dp", "expert"), None),
        P(("dp", "expert"), None),
        P(("dp", "expert"), None),
        P("dp", "expert", None, None, None),
        P("expert", "dp", None),
        P("expert", "dp", None),
        P("expert", "dp"),
    )
    out_specs = (
        P(("dp", "expert"), None, None),
        P("expert", "dp", None),
        P("expert", "dp", None),
        P("expert", "dp"),
    )
    return jax.shard_map(local, mesh=mesh, in_specs=in_specs, out_specs=out_specs, check_vma=False)
```

```python
import functools
import math

import jax
import jax.numpy as jnp
from jax import lax
from jax.experimental import pallas as pl
from jax.experimental.pallas import tpu as pltpu
from jax.sharding import PartitionSpec as P

MESH = pl.DeviceIdType.MESH
bf16 = jnp.bfloat16
f32 = jnp.float32

beta_one = 0.9
beta_two = 0.99
epsilon = 1e-06

D = 2048
FF = 3200
TOK = 256
CAP = 64
HALF = 32
HD = D // 2
ROWS = 80
SHARD = 400
CUT = 208
NCH = 5
C = FF // NCH


def slot_keys(ids):
    tok = ids.shape[1]
    expert = lax.broadcasted_iota(jnp.int32, (16, tok), 0)
    c0 = expert == ids[0:1, :]
    c1 = expert == ids[1:2, :]
    cnt = jnp.where(c0 | c1, 1.0, 0.0).astype(bf16)
    before = jnp.where(
        lax.broadcasted_iota(jnp.int32, (tok, tok), 0) < lax.broadcasted_iota(jnp.int32, (tok, tok), 1), 1.0, 0.0
    ).astype(bf16)
    earlier = jnp.dot(cnt, before, preferred_element_type=f32)
    pos0 = jnp.sum(jnp.where(c0, earlier, 0.0), axis=0, keepdims=True).astype(jnp.int32)
    pos1 = jnp.sum(jnp.where(c1, earlier, 0.0), axis=0, keepdims=True).astype(jnp.int32)
    return ids[0:1, :] * CAP + pos0, ids[1:2, :] * CAP + pos1


def rows_of(start, count):
    return pl.ds(pl.multiple_of(start, 16), count)


def main_kernel(
    factor,
    og, ids, gates, scales, w, hid, codes,
    hidden_grad, direction, new_codes, new_scales,
    ret, pieces, sr, m2a, m2b,
    sa, sb, meta, rr, ww, hv, pb, oo, sums, tt, pk, ost,
    ag_s, ag_r, loc, p1_s, p1_r, mt_s, mt_r, p2_s, p2_r, r1_s, r1_r, r2_s, r2_r, rl, sib_s, sib_r, x_s, x_r, tail_s, own_s,
):
    dp = lax.axis_index("dp")
    ex = lax.axis_index("expert")
    x, c = dp // 2, dp % 2
    y, z = ex // 4, ex % 4

    def dev_x(d):
        return (((x + d) % 4) * 2 + c, ex)

    def dev_y(d):
        return (dp, ((y + d) % 4) * 4 + z)

    def dev_z(d):
        return (dp, y * 4 + (z + d) % 4)

    sibling = (x * 2 + 1 - c, ex)

    barrier = pltpu.get_barrier_semaphore()
    peers = [dev_y(1), dev_y(2), dev_y(3), dev_z(1), dev_z(2), dev_z(3), dev_x(1), dev_x(3), sibling]
    for peer in peers:
        pl.semaphore_signal(barrier, inc=1, device_id=peer, device_id_type=MESH)
    pl.semaphore_wait(barrier, len(peers))

    def remote(src, dst, s, r, device):
        return pltpu.make_async_remote_copy(
            src_ref=src, dst_ref=dst, send_sem=s, recv_sem=r, device_id=device, device_id_type=MESH
        )

    def shard_rows(xx, cc, lo, n):
        return rows_of(((xx % 4) * 2 + cc) * SHARD + lo, n)

    H0 = (0, CUT)
    H1 = (CUT, SHARD - CUT)

    def ag_copy(i, xx, cut, device, own):
        lo, n = cut
        there = ww.at[shard_rows(xx, c, lo, n)]
        src = w.at[pl.ds(lo, n)] if own else there
        return remote(src, there, ag_s.at[i], ag_r.at[i], device)

    ag = [
        ag_copy(0, x, H0, dev_x(1), True),
        ag_copy(1, x, H1, dev_x(1), True),
        ag_copy(2, x, H1, dev_x(3), True),
        ag_copy(3, x, H0, dev_x(3), True),
        ag_copy(4, x + 3, H0, dev_x(1), False),
        ag_copy(5, x + 1, H1, dev_x(3), False),
        ag_copy(6, x, (0, SHARD), sibling, True),
        ag_copy(7, x + 3, H0, sibling, False),
        ag_copy(8, x + 3, H1, sibling, False),
        ag_copy(9, x + 1, H1, sibling, False),
        ag_copy(10, x + 1, H0, sibling, False),
        ag_copy(11, x + 2, H0, sibling, False),
        ag_copy(12, x + 2, H1, sibling, False),
    ]
    w_own = pltpu.make_async_copy(w, ww.at[shard_rows(x, c, 0, SHARD)], loc.at[0])
    for i in (0, 2, 1, 3, 6):
        ag[i].start()
    w_own.start()

    h_load = pltpu.make_async_copy(hid, hv, loc.at[8])
    h_load.start()

    def og_copy(i, own_axis, d, half, axis):
        pos = (y, z)[axis]
        src_pos = (pos + (0, 0, 0, 0, 3, 1)[i]) % 4
        rows = half * (TOK // 2)
        there = pb.at[rows_of(src_pos * TOK + rows, TOK // 2), pl.ds(axis * HD, HD)]
        src = og.at[pl.ds(rows, TOK // 2), pl.ds(axis * HD, HD)] if own_axis else there
        k = axis * 6 + i
        return remote(src, there, p1_s.at[k], p1_r.at[k], (dev_y, dev_z)[axis](d))

    def og_copies(axis):
        return [
            og_copy(0, True, 1, 0, axis),
            og_copy(1, True, 1, 1, axis),
            og_copy(2, True, 3, 1, axis),
            og_copy(3, True, 3, 0, axis),
            og_copy(4, False, 1, 0, axis),
            og_copy(5, False, 3, 1, axis),
        ]

    oy, oz = og_copies(0), og_copies(1)
    for i in (0, 2, 1, 3):
        oy[i].start()
        oz[i].start()

    key0, key1 = slot_keys(ids[...])
    for axis, pos in ((0, y), (1, z)):
        meta[axis * 4 + pos, 0:1, :] = key0.astype(f32)
        meta[axis * 4 + pos, 1:2, :] = key1.astype(f32)
        meta[axis * 4 + pos, 2:4, :] = gates[...]
        meta[axis * 4 + pos, 4:8, :] = jnp.zeros((4, TOK), f32)

    def meta_copy(axis, d):
        at = meta.at[axis * 4 + (y, z)[axis]]
        k = axis * 3 + d - 1
        return remote(at, at, mt_s.at[k], mt_r.at[k], (dev_y, dev_z)[axis](d))

    for d in (1, 3, 2):
        meta_copy(0, d).start()
        meta_copy(1, d).start()

    def build(axis, j):
        pos = ((y, z)[axis] + 4 - j) % 4
        info = meta[axis * 4 + pos]
        i = lax.broadcasted_iota(jnp.int32, (4 * CAP, TOK), 0)
        slot = i + y * (4 * CAP) if axis == 0 else (i // CAP) * (4 * CAP) + z * CAP + i % CAP
        slot = slot.astype(f32)
        e0, e1 = slot == info[0:1], slot == info[1:2]
        pick = jnp.where(e0 | e1, 1.0, 0.0).astype(bf16)
        gate = jnp.sum(jnp.where(e0, info[2:3], 0.0) + jnp.where(e1, info[3:4], 0.0), axis=1, keepdims=True)
        cols = pl.ds(axis * HD, HD)
        rows = og[:, cols] if j == 0 else pb[rows_of(pos * TOK, TOK), cols]
        res = jnp.dot(pick, rows, preferred_element_type=f32)
        (sa, sb)[axis][pos] = (res * gate).astype(bf16).reshape(4, CAP, HD)

    A = pl.ds(0, HALF)
    B = pl.ds(HALF, HALF)
    left, right = pl.ds(0, HD), pl.ds(HD, HD)

    def p2a(j, d):
        sy = (y + 4 - j) % 4
        i = j * 3 + d - 1
        return remote(sa.at[sy, (z + d) % 4], rr.at[sy, z, :, left], p2_s.at[i], p2_r.at[i], dev_z(d))

    def p2b(j, d):
        sz = (z + 4 - j) % 4
        i = 12 + j * 3 + d - 1
        return remote(sb.at[sz, (y + d) % 4], rr.at[y, sz, :, right], p2_s.at[i], p2_r.at[i], dev_y(d))

    def p2a_own(j):
        sy = (y + 4 - j) % 4
        return pltpu.make_async_copy(sa.at[sy, z], rr.at[sy, z, :, left], own_s.at[j])

    def p2b_own(j):
        sz = (z + 4 - j) % 4
        return pltpu.make_async_copy(sb.at[sz, y], rr.at[y, sz, :, right], own_s.at[4 + j])

    def dispatch(j):
        build(0, j)
        for d in (1, 3, 2):
            p2a(j, d).start()
        p2a_own(j).start()
        build(1, j)
        for d in (1, 3, 2):
            p2b(j, d).start()
        p2b_own(j).start()

    dispatch(0)

    oy[0].wait_recv()
    oy[4].start()
    oz[0].wait_recv()
    oz[4].start()
    oy[2].wait_recv()
    oy[5].start()
    oz[2].wait_recv()
    oz[5].start()
    for j, i in ((1, 1), (3, 3)):
        oy[i].wait_recv()
        oz[i].wait_recv()
        meta_copy(0, j).wait_recv()
        meta_copy(1, j).wait_recv()
        dispatch(j)

    slot_id = lax.broadcasted_iota(jnp.int32, (16 * CAP, TOK), 0)
    pk[0:TOK, :] = jnp.where(slot_id == key0, 1.0, 0.0).astype(bf16).T
    pk[TOK:, :] = jnp.where(slot_id == key1, 1.0, 0.0).astype(bf16).T

    for i in (4, 5):
        oy[i].wait_recv()
        oz[i].wait_recv()
    meta_copy(0, 2).wait_recv()
    meta_copy(1, 2).wait_recv()
    dispatch(2)

    ag[0].wait_recv()
    ag[4].start()
    ag[7].start()
    ag[2].wait_recv()
    ag[5].start()
    ag[9].start()
    ag[1].wait_recv()
    ag[8].start()
    ag[3].wait_recv()
    ag[10].start()

    for j in (0, 1, 3, 2):
        for d in (1, 3, 2):
            p2a(j, d).wait_recv()
            p2b(j, d).wait_recv()
        p2a_own(j).wait()
        p2b_own(j).wait()
    for i in range(6):
        oy[i].wait_send()
        oz[i].wait_send()
    w_own.wait()
    for i in range(6, 11):
        ag[i].wait_recv()
    h_load.wait()

    first = ((x + 2) % 4 + 2) % 5

    def chunk(i):
        return (first + i) % NCH

    def product_a(i):
        wj = ww[rows_of(chunk(i) * C, C), :]
        rows = rr[...].reshape(16 * CAP, D)
        res = lax.dot_general(rows, wj, (((1,), (1,)), ((), ())), preferred_element_type=f32)
        oo[i] = res.astype(bf16).reshape(4, 4, CAP, C)

    def product_b(i):
        at = chunk(i) * C

        def part(n, carry):
            cols = pl.ds(pl.multiple_of(n * 1024, 1024), 1024)
            hj = hv[:, pl.ds(pl.multiple_of(at, 128), C)]
            rows = rr[:, :, :, cols].reshape(16 * CAP, 1024)
            res = lax.dot_general(hj, rows, (((0,), (0,)), ((), ())), preferred_element_type=f32)
            pb[rows_of(at, C), cols] = res.astype(bf16)
            return carry

        lax.fori_loop(0, D // 1024, part, 0)

    def r1a(j, d):
        return remote(oo.at[j, (y + d) % 4, :, A, :], m2a.at[j, y], r1_s.at[j, d - 1], r1_r.at[j, d - 1], dev_y(d))

    def r1b(j, d):
        return remote(oo.at[j, :, (z + d) % 4, B, :], m2b.at[j, z], r1_s.at[j, 2 + d], r1_r.at[j, 2 + d], dev_z(d))

    def r1a_own(j):
        return pltpu.make_async_copy(oo.at[j, y, :, A, :], m2a.at[j, y], rl.at[j, 0])

    def r1b_own(j):
        return pltpu.make_async_copy(oo.at[j, :, z, B, :], m2b.at[j, z], rl.at[j, 1])

    def r2a(j, d):
        return remote(
            m2a.at[j, :, (z + d) % 4], ret.at[chunk(j), :, z, A, :], r2_s.at[j, d - 1], r2_r.at[j, d - 1], dev_z(d)
        )

    def r2b(j, d):
        return remote(
            m2b.at[j, :, (y + d) % 4], ret.at[chunk(j), y, :, B, :], r2_s.at[j, 2 + d], r2_r.at[j, 2 + d], dev_y(d)
        )

    def r2a_own(j):
        return pltpu.make_async_copy(m2a.at[j, :, z], ret.at[chunk(j), :, z, A, :], rl.at[j, 2])

    def r2b_own(j):
        return pltpu.make_async_copy(m2b.at[j, :, y], ret.at[chunk(j), y, :, B, :], rl.at[j, 3])

    def send(j):
        for d in (1, 3, 2):
            r1a(j, d).start()
            r1b(j, d).start()
        r1a_own(j).start()
        r1b_own(j).start()

    def forward(j):
        r1a_own(j).wait()
        for d in (1, 3, 2):
            r1a(j, d).wait_recv()
        for d in (1, 3, 2):
            r2a(j, d).start()
        r2a_own(j).start()
        r1b_own(j).wait()
        for d in (1, 3, 2):
            r1b(j, d).wait_recv()
        for d in (1, 3, 2):
            r2b(j, d).start()
        r2b_own(j).start()

    hop = (2, 1, 3, 0)

    def to_sibling(k):
        return remote(pb.at[shard_rows(x + hop[k], 1 - c, 0, SHARD)], sr.at[k], sib_s.at[k], sib_r.at[k], sibling)

    def add_sibling(k):
        to_sibling(k).wait_recv()
        load = pltpu.make_async_copy(sr.at[k], sums, loc.at[7])
        load.start()
        load.wait()

        def part(i, carry):
            at = shard_rows(x + hop[k], c, i * 80, 80)
            mine = pb[at, :].astype(f32) + sums[rows_of(i * 80, 80), :].astype(f32)
            pb[at, :] = mine.astype(bf16)
            return carry

        lax.fori_loop(0, SHARD // 80, part, 0)

    def far(i):
        lo, n = (H0, H1)[i]
        return remote(
            pb.at[shard_rows(x + 2, c, lo, n)], tt.at[pl.ds(lo, n)], x_s.at[i], x_r.at[i], dev_x((1, 3)[i])
        )

    def add_far(i):
        far(i).wait_recv()
        lo, n = (H0, H1)[i]

        def part(k, carry):
            at = shard_rows(x + (1, 3)[i], c, lo + k * 16, 16)
            mine = pb[at, :].astype(f32) + tt[pl.ds(pl.multiple_of(lo + k * 16, 16), 16), :].astype(f32)
            pb[at, :] = mine.astype(bf16)
            return carry

        lax.fori_loop(0, n // 16, part, 0)

    def near(i, h):
        lo, n = (H0, H1)[h]
        k = 2 + 2 * i + h
        return remote(
            pb.at[shard_rows(x + (1, 3)[i], c, lo, n)],
            pieces.at[i, pl.ds(lo, n)],
            x_s.at[k],
            x_r.at[k],
            dev_x((1, 3)[i]),
        )

    def stage(i):
        buf, at = ((sa, 0), (sb, 0), (rr, 0), (rr, 1), (rr, 2))[i]
        return buf.at[:, :, :, pl.ds(at * C, C)]

    def stage_load(i):
        return pltpu.make_async_copy(ret.at[chunk(i)], stage(i), tail_s.at[i])

    def out_copy(i):
        at = pl.ds(pl.multiple_of(chunk(i) * C, 128), C)
        return pltpu.make_async_copy(ost.at[i % 2], hidden_grad.at[:, :, at], tail_s.at[NCH + i])

    def pick(i):
        r2a_own(i).wait()
        r2b_own(i).wait()
        for d in (1, 3, 2):
            r2a(i, d).wait_recv()
            r2b(i, d).wait_recv()
        stage_load(i).start()
        stage_load(i).wait()
        if i >= 2:
            out_copy(i - 2).wait()
        rows = stage(i)[...].reshape(16 * CAP, C)
        got = jnp.dot(pk[...], rows, preferred_element_type=f32).astype(bf16)
        ost[i % 2, :, 0, :] = got[0:TOK]
        ost[i % 2, :, 1, :] = got[TOK:]
        out_copy(i).start()

    def step_load(k):
        src = (codes, pieces.at[0], pieces.at[1])[k]
        return pltpu.make_async_copy(src, ww.at[pl.ds(k * SHARD, SHARD)], tail_s.at[2 * NCH + k])

    def step_out(k):
        dst = (new_codes, direction)[k]
        return pltpu.make_async_copy(ww.at[pl.ds(k * SHARD, SHARD)], dst, tail_s.at[2 * NCH + 3 + k])

    def step():
        for k in range(3):
            step_load(k).wait()
        new_scales[...] = jnp.zeros_like(new_scales)

        def part(i, carry):
            def of(k):
                return ww[rows_of(k * SHARD + i * ROWS, ROWS), :].astype(f32)

            mine = pb[shard_rows(x, c, i * ROWS, ROWS), :].astype(f32)
            gradient = factor * (mine + of(1) + of(2))
            here = lax.broadcasted_iota(jnp.int32, (ROWS, SHARD), 0) + i * ROWS == lax.broadcasted_iota(
                jnp.int32, (ROWS, SHARD), 1
            )
            scale = jnp.sum(jnp.where(here, scales[...], 0.0), axis=1, keepdims=True)
            momentum = of(0) * scale
            blended = beta_one * momentum + (1.0 - beta_one) * gradient
            root = lax.rsqrt(jnp.mean(blended * blended, axis=-1, keepdims=True) + epsilon)
            advanced = beta_two * momentum + (1.0 - beta_two) * gradient
            largest = jnp.max(jnp.abs(advanced), axis=-1, keepdims=True) + epsilon
            ww[rows_of(SHARD + i * ROWS, ROWS), :] = jnp.tanh(blended * root).astype(bf16)
            ww[rows_of(i * ROWS, ROWS), :] = (advanced * (1.0 / largest)).astype(bf16)
            new_scales[...] += jnp.sum(jnp.where(here, largest, 0.0), axis=0, keepdims=True)
            return carry

        lax.fori_loop(0, SHARD // ROWS, part, 0)
        for k in range(2):
            step_out(k).start()

    product_a(0)
    send(0)
    product_b(3)
    product_b(4)
    to_sibling(0).start()
    forward(0)
    ag[4].wait_recv()
    ag[11].start()
    ag[5].wait_recv()
    ag[12].start()
    product_a(1)
    send(1)
    add_sibling(0)
    far(0).start()
    far(1).start()
    product_a(2)
    send(2)
    product_b(0)
    forward(1)
    product_b(1)
    product_b(2)
    for k in range(1, 4):
        to_sibling(k).start()
    ag[11].wait_recv()
    ag[12].wait_recv()
    product_a(3)
    send(3)
    add_sibling(1)
    near(0, 1).start()
    add_sibling(2)
    near(1, 0).start()
    forward(2)
    add_far(0)
    near(0, 0).start()
    add_far(1)
    near(1, 1).start()
    product_a(4)
    send(4)
    add_sibling(3)

    for i in range(13):
        ag[i].wait_send()
    for d in (1, 2, 3):
        meta_copy(0, d).wait_send()
        meta_copy(1, d).wait_send()
        for j in range(4):
            p2a(j, d).wait_send()
            p2b(j, d).wait_send()
    step_load(0).start()

    pick(0)
    forward(3)
    pick(1)
    forward(4)
    pick(2)
    for i in range(2):
        for h in range(2):
            near(i, h).wait_recv()
    step_load(1).start()
    step_load(2).start()
    pick(3)
    step()
    pick(4)

    for k in range(4):
        to_sibling(k).wait_send()
    for i in range(2):
        far(i).wait_send()
        for h in range(2):
            near(i, h).wait_send()
    for j in range(NCH):
        for d in (1, 2, 3):
            r1a(j, d).wait_send()
            r1b(j, d).wait_send()
            r2a(j, d).wait_send()
            r2b(j, d).wait_send()
    for k in range(2):
        step_out(k).wait()
    out_copy(3).wait()
    out_copy(4).wait()


def main_call(factor, og, ids, gates, scales, w, hid, codes):
    any_spec = pl.BlockSpec(memory_space=pl.ANY)
    vmem = pl.BlockSpec(memory_space=pltpu.VMEM)
    dma = pltpu.SemaphoreType.DMA
    s = jax.ShapeDtypeStruct
    return pl.pallas_call(
        functools.partial(main_kernel, factor),
        out_shape=(
            s((TOK, 2, FF), bf16),
            s((SHARD, D), bf16),
            s((SHARD, D), bf16),
            s((1, SHARD), f32),
            s((NCH, 4, 4, CAP, C), bf16),
            s((2, SHARD, D), bf16),
            s((4, SHARD, D), bf16),
            s((NCH, 4, 4, HALF, C), bf16),
            s((NCH, 4, 4, HALF, C), bf16),
        ),
        in_specs=[vmem] * 4 + [any_spec] * 3,
        out_specs=[any_spec] * 3 + [vmem] + [any_spec] * 5,
        scratch_shapes=[
            pltpu.VMEM((4, 4, CAP, HD), bf16),
            pltpu.VMEM((4, 4, CAP, HD), bf16),
            pltpu.VMEM((8, 8, TOK), f32),
            pltpu.VMEM((4, 4, CAP, D), bf16),
            pltpu.VMEM((FF, D), bf16),
            pltpu.VMEM((16 * CAP, FF), bf16),
            pltpu.VMEM((FF, D), bf16),
            pltpu.VMEM((NCH, 4, 4, CAP, C), bf16),
            pltpu.VMEM((SHARD, D), bf16),
            pltpu.VMEM((SHARD, D), bf16),
            pltpu.VMEM((2 * TOK, 16 * CAP), bf16),
            pltpu.VMEM((2, TOK, 2, C), bf16),
            dma((13,)), dma((13,)), dma((9,)),
            dma((12,)), dma((12,)), dma((6,)), dma((6,)), dma((24,)), dma((24,)),
            dma((NCH, 6)), dma((NCH, 6)), dma((NCH, 6)), dma((NCH, 6)), dma((NCH, 4)),
            dma((4,)), dma((4,)), dma((6,)), dma((6,)), dma((2 * NCH + 5,)), dma((8,)),
        ],
        compiler_params=pltpu.CompilerParams(
            collective_id=0, has_side_effects=True, vmem_limit_bytes=63 * 2**20
        ),
        cost_estimate=pl.CostEstimate(flops=32 * 10**9, bytes_accessed=60 * 10**6, transcendentals=0),
        name="expert_backward",
    )(og, ids, gates, scales, w, hid, codes)


def place_kernel(grad, direction, codes, scales, grad_out, direction_out, codes_out, scales_out):
    grad_out[...] = grad[...]
    direction_out[...] = direction[...]
    codes_out[...] = codes[...]
    scales_out[...] = scales[...]


def place_call(*arrays):
    blocks = [
        pl.BlockSpec((TOK // 8, 2, FF), lambda i: (i, 0, 0)),
        pl.BlockSpec((SHARD, D // 8), lambda i: (0, i)),
        pl.BlockSpec((SHARD, D // 8), lambda i: (0, i)),
        pl.BlockSpec((1, SHARD), lambda i: (0, 0)),
    ]
    return pl.pallas_call(
        place_kernel,
        grid=(8,),
        out_shape=tuple(jax.ShapeDtypeStruct(a.shape, a.dtype) for a in arrays),
        in_specs=blocks,
        out_specs=blocks,
        name="place_outputs",
    )(*arrays)


def local(out_grad, expert_ids, gates, hidden_slots, weights, mom_codes, mom_scales):
    experts = lax.axis_size("expert")
    groups = lax.axis_size("dp")
    tokens_all = out_grad.shape[0] * groups * experts
    ids = expert_ids.T
    factor = math.sqrt(experts / (2.0 * tokens_all))
    results = main_call(
        factor, out_grad, ids, gates.T, mom_scales, weights[0], hidden_slots.reshape(16 * CAP, FF), mom_codes[0]
    )[:4]
    hidden_grad, direction, new_codes, new_scales = place_call(*results)
    return (hidden_grad, direction[None], new_codes[None], new_scales)


def solution(mesh):
    in_specs = (
        P(("dp", "expert"), None),
        P(("dp", "expert"), None),
        P(("dp", "expert"), None),
        P("dp", "expert", None, None, None),
        P("expert", "dp", None),
        P("expert", "dp", None),
        P("expert", "dp"),
    )
    out_specs = (
        P(("dp", "expert"), None, None),
        P("expert", "dp", None),
        P("expert", "dp", None),
        P("expert", "dp"),
    )
    return jax.shard_map(local, mesh=mesh, in_specs=in_specs, out_specs=out_specs, check_vma=False)
```

```python
import functools
import math

import jax
import jax.numpy as jnp
from jax import lax
from jax.experimental import pallas as pl
from jax.experimental.pallas import tpu as pltpu
from jax.sharding import PartitionSpec as P

MESH = pl.DeviceIdType.MESH
bf16 = jnp.bfloat16
f32 = jnp.float32

beta_one = 0.9
beta_two = 0.99
epsilon = 1e-06

D = 2048
FF = 3200
TOK = 256
CAP = 64
HALF = 32
HD = D // 2
ROWS = 80
SHARD = 400
CUT = 208
NCH = 5
C = FF // NCH


def slot_keys(ids):
    tok = ids.shape[1]
    expert = lax.broadcasted_iota(jnp.int32, (16, tok), 0)
    c0 = expert == ids[0:1, :]
    c1 = expert == ids[1:2, :]
    cnt = jnp.where(c0 | c1, 1.0, 0.0).astype(bf16)
    before = jnp.where(
        lax.broadcasted_iota(jnp.int32, (tok, tok), 0) < lax.broadcasted_iota(jnp.int32, (tok, tok), 1), 1.0, 0.0
    ).astype(bf16)
    earlier = jnp.dot(cnt, before, preferred_element_type=f32)
    pos0 = jnp.sum(jnp.where(c0, earlier, 0.0), axis=0, keepdims=True).astype(jnp.int32)
    pos1 = jnp.sum(jnp.where(c1, earlier, 0.0), axis=0, keepdims=True).astype(jnp.int32)
    return ids[0:1, :] * CAP + pos0, ids[1:2, :] * CAP + pos1


def rows_of(start, count):
    return pl.ds(pl.multiple_of(start, 16), count)


def main_kernel(
    factor,
    og, ids, gates, scales, w, hid, codes,
    hidden_grad, direction, new_codes, new_scales,
    ret, pieces, sr, m2a, m2b,
    sa, sb, meta, rr, ww, hv, pb, oo, sums, tt, pk, ost, last,
    ag_s, ag_r, loc, p1_s, p1_r, mt_s, mt_r, p2_s, p2_r, r1_s, r1_r, r2_s, r2_r, rl, sib_s, sib_r, x_s, x_r, tail_s, own_s,
):
    dp = lax.axis_index("dp")
    ex = lax.axis_index("expert")
    x, c = dp // 2, dp % 2
    y, z = ex // 4, ex % 4

    def dev_x(d):
        return (((x + d) % 4) * 2 + c, ex)

    def dev_y(d):
        return (dp, ((y + d) % 4) * 4 + z)

    def dev_z(d):
        return (dp, y * 4 + (z + d) % 4)

    sibling = (x * 2 + 1 - c, ex)

    barrier = pltpu.get_barrier_semaphore()
    peers = [dev_y(1), dev_y(2), dev_y(3), dev_z(1), dev_z(2), dev_z(3), dev_x(1), dev_x(3), sibling]
    for peer in peers:
        pl.semaphore_signal(barrier, inc=1, device_id=peer, device_id_type=MESH)
    pl.semaphore_wait(barrier, len(peers))

    def remote(src, dst, s, r, device):
        return pltpu.make_async_remote_copy(
            src_ref=src, dst_ref=dst, send_sem=s, recv_sem=r, device_id=device, device_id_type=MESH
        )

    def shard_rows(xx, cc, lo, n):
        return rows_of(((xx % 4) * 2 + cc) * SHARD + lo, n)

    H0 = (0, CUT)
    H1 = (CUT, SHARD - CUT)

    def ag_copy(i, xx, cut, device, own):
        lo, n = cut
        there = ww.at[shard_rows(xx, c, lo, n)]
        src = w.at[pl.ds(lo, n)] if own else there
        return remote(src, there, ag_s.at[i], ag_r.at[i], device)

    ag = [
        ag_copy(0, x, H0, dev_x(1), True),
        ag_copy(1, x, H1, dev_x(1), True),
        ag_copy(2, x, H1, dev_x(3), True),
        ag_copy(3, x, H0, dev_x(3), True),
        ag_copy(4, x + 3, H0, dev_x(1), False),
        ag_copy(5, x + 1, H1, dev_x(3), False),
        ag_copy(6, x, (0, SHARD), sibling, True),
        ag_copy(7, x + 3, H0, sibling, False),
        ag_copy(8, x + 3, H1, sibling, False),
        ag_copy(9, x + 1, H1, sibling, False),
        ag_copy(10, x + 1, H0, sibling, False),
        ag_copy(11, x + 2, H0, sibling, False),
        ag_copy(12, x + 2, H1, sibling, False),
    ]
    w_own = pltpu.make_async_copy(w, ww.at[shard_rows(x, c, 0, SHARD)], loc.at[0])
    for i in (0, 2, 1, 3, 6):
        ag[i].start()
    w_own.start()

    h_load = pltpu.make_async_copy(hid, hv, loc.at[8])
    h_load.start()

    def og_copy(i, own_axis, d, half, axis):
        pos = (y, z)[axis]
        src_pos = (pos + (0, 0, 0, 0, 3, 1)[i]) % 4
        rows = half * (TOK // 2)
        there = pb.at[rows_of(src_pos * TOK + rows, TOK // 2), pl.ds(axis * HD, HD)]
        src = og.at[pl.ds(rows, TOK // 2), pl.ds(axis * HD, HD)] if own_axis else there
        k = axis * 6 + i
        return remote(src, there, p1_s.at[k], p1_r.at[k], (dev_y, dev_z)[axis](d))

    def og_copies(axis):
        return [
            og_copy(0, True, 1, 0, axis),
            og_copy(1, True, 1, 1, axis),
            og_copy(2, True, 3, 1, axis),
            og_copy(3, True, 3, 0, axis),
            og_copy(4, False, 1, 0, axis),
            og_copy(5, False, 3, 1, axis),
        ]

    oy, oz = og_copies(0), og_copies(1)
    for i in (0, 2, 1, 3):
        oy[i].start()
        oz[i].start()

    key0, key1 = slot_keys(ids[...])
    for axis, pos in ((0, y), (1, z)):
        meta[axis * 4 + pos, 0:1, :] = key0.astype(f32)
        meta[axis * 4 + pos, 1:2, :] = key1.astype(f32)
        meta[axis * 4 + pos, 2:4, :] = gates[...]
        meta[axis * 4 + pos, 4:8, :] = jnp.zeros((4, TOK), f32)

    def meta_copy(axis, d):
        at = meta.at[axis * 4 + (y, z)[axis]]
        k = axis * 3 + d - 1
        return remote(at, at, mt_s.at[k], mt_r.at[k], (dev_y, dev_z)[axis](d))

    for d in (1, 3, 2):
        meta_copy(0, d).start()
        meta_copy(1, d).start()

    def build(axis, j):
        pos = ((y, z)[axis] + 4 - j) % 4
        info = meta[axis * 4 + pos]
        i = lax.broadcasted_iota(jnp.int32, (4 * CAP, TOK), 0)
        slot = i + y * (4 * CAP) if axis == 0 else (i // CAP) * (4 * CAP) + z * CAP + i % CAP
        slot = slot.astype(f32)
        e0, e1 = slot == info[0:1], slot == info[1:2]
        pick = jnp.where(e0 | e1, 1.0, 0.0).astype(bf16)
        gate = jnp.sum(jnp.where(e0, info[2:3], 0.0) + jnp.where(e1, info[3:4], 0.0), axis=1, keepdims=True)
        cols = pl.ds(axis * HD, HD)
        rows = og[:, cols] if j == 0 else pb[rows_of(pos * TOK, TOK), cols]
        res = jnp.dot(pick, rows, preferred_element_type=f32)
        (sa, sb)[axis][pos] = (res * gate).astype(bf16).reshape(4, CAP, HD)

    A = pl.ds(0, HALF)
    B = pl.ds(HALF, HALF)
    left, right = pl.ds(0, HD), pl.ds(HD, HD)

    def p2a(j, d):
        sy = (y + 4 - j) % 4
        i = j * 3 + d - 1
        return remote(sa.at[sy, (z + d) % 4], rr.at[sy, z, :, left], p2_s.at[i], p2_r.at[i], dev_z(d))

    def p2b(j, d):
        sz = (z + 4 - j) % 4
        i = 12 + j * 3 + d - 1
        return remote(sb.at[sz, (y + d) % 4], rr.at[y, sz, :, right], p2_s.at[i], p2_r.at[i], dev_y(d))

    def p2a_own(j):
        sy = (y + 4 - j) % 4
        return pltpu.make_async_copy(sa.at[sy, z], rr.at[sy, z, :, left], own_s.at[j])

    def p2b_own(j):
        sz = (z + 4 - j) % 4
        return pltpu.make_async_copy(sb.at[sz, y], rr.at[y, sz, :, right], own_s.at[4 + j])

    def dispatch(j):
        build(0, j)
        for d in (1, 3, 2):
            p2a(j, d).start()
        p2a_own(j).start()
        build(1, j)
        for d in (1, 3, 2):
            p2b(j, d).start()
        p2b_own(j).start()

    dispatch(0)

    oy[0].wait_recv()
    oy[4].start()
    oz[0].wait_recv()
    oz[4].start()
    oy[2].wait_recv()
    oy[5].start()
    oz[2].wait_recv()
    oz[5].start()
    for j, i in ((1, 1), (3, 3)):
        oy[i].wait_recv()
        oz[i].wait_recv()
        meta_copy(0, j).wait_recv()
        meta_copy(1, j).wait_recv()
        dispatch(j)

    slot_id = lax.broadcasted_iota(jnp.int32, (16 * CAP, TOK), 0)
    pk[0:TOK, :] = jnp.where(slot_id == key0, 1.0, 0.0).astype(bf16).T
    pk[TOK:, :] = jnp.where(slot_id == key1, 1.0, 0.0).astype(bf16).T

    for i in (4, 5):
        oy[i].wait_recv()
        oz[i].wait_recv()
    meta_copy(0, 2).wait_recv()
    meta_copy(1, 2).wait_recv()
    dispatch(2)

    ag[0].wait_recv()
    ag[4].start()
    ag[7].start()
    ag[2].wait_recv()
    ag[5].start()
    ag[9].start()
    ag[1].wait_recv()
    ag[8].start()
    ag[3].wait_recv()
    ag[10].start()

    w_own.wait()
    for i in range(6, 11):
        ag[i].wait_recv()
    h_load.wait()

    def rows_here(d):
        for k in (1, 3, 2):
            p2a((4 - d) % 4, k).wait_recv()
        p2a_own((4 - d) % 4).wait()
        for j in (0, 1, 3, 2):
            if d:
                p2b(j, 4 - d).wait_recv()
            else:
                p2b_own(j).wait()

    first = ((x + 2) % 4 + 2) % 5

    def chunk(i):
        return (first + i) % NCH

    def product_a(i):
        wj = ww[rows_of(chunk(i) * C, C), :]
        rows = rr[...].reshape(16 * CAP, D)
        res = lax.dot_general(rows, wj, (((1,), (1,)), ((), ())), preferred_element_type=f32)
        oo[i] = res.astype(bf16).reshape(4, 4, CAP, C)

    def product_first(d):
        sy = (y + d) % 4
        wj = ww[rows_of(chunk(0) * C, C), :]
        rows = rr[sy].reshape(4 * CAP, D)
        res = lax.dot_general(rows, wj, (((1,), (1,)), ((), ())), preferred_element_type=f32)
        oo[0, sy] = res.astype(bf16).reshape(4, CAP, C)

    def product_b(i):
        at = chunk(i) * C

        def part(n, carry):
            cols = pl.ds(pl.multiple_of(n * 1024, 1024), 1024)
            hj = hv[:, pl.ds(pl.multiple_of(at, 128), C)]
            rows = rr[:, :, :, cols].reshape(16 * CAP, 1024)
            res = lax.dot_general(hj, rows, (((0,), (0,)), ((), ())), preferred_element_type=f32)
            pb[rows_of(at, C), cols] = res.astype(bf16)
            return carry

        lax.fori_loop(0, D // 1024, part, 0)

    def r1a(j, d):
        return remote(oo.at[j, (y + d) % 4, :, A, :], m2a.at[j, y], r1_s.at[j, d - 1], r1_r.at[j, d - 1], dev_y(d))

    def r1b(j, d):
        return remote(oo.at[j, :, (z + d) % 4, B, :], m2b.at[j, z], r1_s.at[j, 2 + d], r1_r.at[j, 2 + d], dev_z(d))

    def r1a_own(j):
        return pltpu.make_async_copy(oo.at[j, y, :, A, :], m2a.at[j, y], rl.at[j, 0])

    def r1b_own(j):
        return pltpu.make_async_copy(oo.at[j, :, z, B, :], m2b.at[j, z], rl.at[j, 1])

    def back(j):
        return last if j == NCH - 1 else ret.at[chunk(j)]

    def r2a(j, d):
        return remote(
            m2a.at[j, :, (z + d) % 4], back(j).at[:, z, A, :], r2_s.at[j, d - 1], r2_r.at[j, d - 1], dev_z(d)
        )

    def r2b(j, d):
        return remote(
            m2b.at[j, :, (y + d) % 4], back(j).at[y, :, B, :], r2_s.at[j, 2 + d], r2_r.at[j, 2 + d], dev_y(d)
        )

    def r2a_own(j):
        return pltpu.make_async_copy(m2a.at[j, :, z], back(j).at[:, z, A, :], rl.at[j, 2])

    def r2b_own(j):
        return pltpu.make_async_copy(m2b.at[j, :, y], back(j).at[y, :, B, :], rl.at[j, 3])

    def send(j):
        for d in (1, 3, 2):
            r1a(j, d).start()
            r1b(j, d).start()
        r1a_own(j).start()
        r1b_own(j).start()

    def forward(j):
        r1a_own(j).wait()
        for d in (1, 3, 2):
            r1a(j, d).wait_recv()
        for d in (1, 3, 2):
            r2a(j, d).start()
        r2a_own(j).start()
        r1b_own(j).wait()
        for d in (1, 3, 2):
            r1b(j, d).wait_recv()
        for d in (1, 3, 2):
            r2b(j, d).start()
        r2b_own(j).start()

    hop = (2, 1, 3, 0)

    def to_sibling(k):
        return remote(pb.at[shard_rows(x + hop[k], 1 - c, 0, SHARD)], sr.at[k], sib_s.at[k], sib_r.at[k], sibling)

    def add_sibling(k):
        to_sibling(k).wait_recv()
        load = pltpu.make_async_copy(sr.at[k], sums, loc.at[7])
        load.start()
        load.wait()

        def part(i, carry):
            at = shard_rows(x + hop[k], c, i * 80, 80)
            mine = pb[at, :].astype(f32) + sums[rows_of(i * 80, 80), :].astype(f32)
            pb[at, :] = mine.astype(bf16)
            return carry

        lax.fori_loop(0, SHARD // 80, part, 0)

    def far(i):
        lo, n = (H0, H1)[i]
        return remote(
            pb.at[shard_rows(x + 2, c, lo, n)], tt.at[pl.ds(lo, n)], x_s.at[i], x_r.at[i], dev_x((1, 3)[i])
        )

    def add_far(i):
        far(i).wait_recv()
        lo, n = (H0, H1)[i]

        def part(k, carry):
            at = shard_rows(x + (1, 3)[i], c, lo + k * 16, 16)
            mine = pb[at, :].astype(f32) + tt[pl.ds(pl.multiple_of(lo + k * 16, 16), 16), :].astype(f32)
            pb[at, :] = mine.astype(bf16)
            return carry

        lax.fori_loop(0, n // 16, part, 0)

    def near(i, h):
        lo, n = (H0, H1)[h]
        k = 2 + 2 * i + h
        return remote(
            pb.at[shard_rows(x + (1, 3)[i], c, lo, n)],
            pieces.at[i, pl.ds(lo, n)],
            x_s.at[k],
            x_r.at[k],
            dev_x((1, 3)[i]),
        )

    def stage(i):
        buf, at = ((sa, 0), (sb, 0), (rr, 0), (rr, 1), (rr, 2))[i]
        return buf.at[:, :, :, pl.ds(at * C, C)]

    def stage_load(i):
        return pltpu.make_async_copy(ret.at[chunk(i)], stage(i), tail_s.at[i])

    def out_copy(i):
        at = pl.ds(pl.multiple_of(chunk(i) * C, 128), C)
        return pltpu.make_async_copy(ost.at[i % 2], hidden_grad.at[:, :, at], tail_s.at[NCH + i])

    def pick(i):
        r2a_own(i).wait()
        r2b_own(i).wait()
        for d in (1, 3, 2):
            r2a(i, d).wait_recv()
            r2b(i, d).wait_recv()
        if i < NCH - 1:
            stage_load(i).start()
            stage_load(i).wait()
        if i >= 2:
            out_copy(i - 2).wait()
        rows = (last if i == NCH - 1 else stage(i))[...].reshape(16 * CAP, C)
        got = jnp.dot(pk[...], rows, preferred_element_type=f32).astype(bf16)
        ost[i % 2, :, 0, :] = got[0:TOK]
        ost[i % 2, :, 1, :] = got[TOK:]
        out_copy(i).start()

    def step_load(k):
        src = (codes, pieces.at[0], pieces.at[1])[k]
        return pltpu.make_async_copy(src, ww.at[pl.ds(k * SHARD, SHARD)], tail_s.at[2 * NCH + k])

    def step_out(k):
        dst = (new_codes, direction)[k]
        return pltpu.make_async_copy(ww.at[pl.ds(k * SHARD, SHARD)], dst, tail_s.at[2 * NCH + 3 + k])

    def step():
        for k in range(3):
            step_load(k).wait()
        new_scales[...] = jnp.zeros_like(new_scales)

        def part(i, carry):
            def of(k):
                return ww[rows_of(k * SHARD + i * ROWS, ROWS), :].astype(f32)

            mine = pb[shard_rows(x, c, i * ROWS, ROWS), :].astype(f32)
            gradient = factor * (mine + of(1) + of(2))
            here = lax.broadcasted_iota(jnp.int32, (ROWS, SHARD), 0) + i * ROWS == lax.broadcasted_iota(
                jnp.int32, (ROWS, SHARD), 1
            )
            scale = jnp.sum(jnp.where(here, scales[...], 0.0), axis=1, keepdims=True)
            momentum = of(0) * scale
            blended = beta_one * momentum + (1.0 - beta_one) * gradient
            root = lax.rsqrt(jnp.mean(blended * blended, axis=-1, keepdims=True) + epsilon)
            advanced = beta_two * momentum + (1.0 - beta_two) * gradient
            largest = jnp.max(jnp.abs(advanced), axis=-1, keepdims=True) + epsilon
            ww[rows_of(SHARD + i * ROWS, ROWS), :] = jnp.tanh(blended * root).astype(bf16)
            ww[rows_of(i * ROWS, ROWS), :] = (advanced * (1.0 / largest)).astype(bf16)
            new_scales[...] += jnp.sum(jnp.where(here, largest, 0.0), axis=0, keepdims=True)
            return carry

        lax.fori_loop(0, SHARD // ROWS, part, 0)
        for k in range(2):
            step_out(k).start()

    rows_here(0)
    product_first(0)
    r1a_own(0).start()
    for d in (1, 3, 2):
        rows_here(d)
        product_first(d)
        r1a(0, d).start()
    for d in (1, 3, 2):
        r1b(0, d).start()
    r1b_own(0).start()
    for i in range(6):
        oy[i].wait_send()
        oz[i].wait_send()
    product_b(3)
    product_a(1)
    send(1)
    product_b(4)
    to_sibling(0).start()
    forward(0)
    ag[4].wait_recv()
    ag[11].start()
    ag[5].wait_recv()
    ag[12].start()
    product_b(0)
    add_sibling(0)
    far(0).start()
    far(1).start()
    product_b(1)
    product_b(2)
    for k in range(1, 4):
        to_sibling(k).start()
    product_a(2)
    send(2)
    forward(1)
    add_sibling(1)
    near(0, 1).start()
    add_sibling(2)
    near(1, 0).start()
    ag[11].wait_recv()
    ag[12].wait_recv()
    product_a(3)
    send(3)
    add_far(0)
    near(0, 0).start()
    add_far(1)
    near(1, 1).start()
    product_a(4)
    send(4)
    forward(2)
    add_sibling(3)

    for i in range(13):
        ag[i].wait_send()
    for d in (1, 2, 3):
        meta_copy(0, d).wait_send()
        meta_copy(1, d).wait_send()
        for j in range(4):
            p2a(j, d).wait_send()
            p2b(j, d).wait_send()
    step_load(0).start()

    pick(0)
    forward(3)
    pick(1)
    forward(4)
    pick(2)
    for i in range(2):
        for h in range(2):
            near(i, h).wait_recv()
    step_load(1).start()
    step_load(2).start()
    pick(3)
    step()
    pick(4)

    for k in range(4):
        to_sibling(k).wait_send()
    for i in range(2):
        far(i).wait_send()
        for h in range(2):
            near(i, h).wait_send()
    for j in range(NCH):
        for d in (1, 2, 3):
            r1a(j, d).wait_send()
            r1b(j, d).wait_send()
            r2a(j, d).wait_send()
            r2b(j, d).wait_send()
    for k in range(2):
        step_out(k).wait()
    out_copy(3).wait()
    out_copy(4).wait()


def main_call(factor, og, ids, gates, scales, w, hid, codes):
    any_spec = pl.BlockSpec(memory_space=pl.ANY)
    vmem = pl.BlockSpec(memory_space=pltpu.VMEM)
    dma = pltpu.SemaphoreType.DMA
    s = jax.ShapeDtypeStruct
    return pl.pallas_call(
        functools.partial(main_kernel, factor),
        out_shape=(
            s((TOK, 2, FF), bf16),
            s((SHARD, D), bf16),
            s((SHARD, D), bf16),
            s((1, SHARD), f32),
            s((NCH, 4, 4, CAP, C), bf16),
            s((2, SHARD, D), bf16),
            s((4, SHARD, D), bf16),
            s((NCH, 4, 4, HALF, C), bf16),
            s((NCH, 4, 4, HALF, C), bf16),
        ),
        in_specs=[vmem] * 4 + [any_spec] * 3,
        out_specs=[any_spec] * 3 + [vmem] + [any_spec] * 5,
        scratch_shapes=[
            pltpu.VMEM((4, 4, CAP, HD), bf16),
            pltpu.VMEM((4, 4, CAP, HD), bf16),
            pltpu.VMEM((8, 8, TOK), f32),
            pltpu.VMEM((4, 4, CAP, D), bf16),
            pltpu.VMEM((FF, D), bf16),
            pltpu.VMEM((16 * CAP, FF), bf16),
            pltpu.VMEM((FF, D), bf16),
            pltpu.VMEM((NCH, 4, 4, CAP, C), bf16),
            pltpu.VMEM((SHARD, D), bf16),
            pltpu.VMEM((SHARD, D), bf16),
            pltpu.VMEM((2 * TOK, 16 * CAP), bf16),
            pltpu.VMEM((2, TOK, 2, C), bf16),
            pltpu.VMEM((4, 4, CAP, C), bf16),
            dma((13,)), dma((13,)), dma((9,)),
            dma((12,)), dma((12,)), dma((6,)), dma((6,)), dma((24,)), dma((24,)),
            dma((NCH, 6)), dma((NCH, 6)), dma((NCH, 6)), dma((NCH, 6)), dma((NCH, 4)),
            dma((4,)), dma((4,)), dma((6,)), dma((6,)), dma((2 * NCH + 5,)), dma((8,)),
        ],
        compiler_params=pltpu.CompilerParams(
            collective_id=0, has_side_effects=True, vmem_limit_bytes=63 * 2**20
        ),
        cost_estimate=pl.CostEstimate(flops=32 * 10**9, bytes_accessed=60 * 10**6, transcendentals=0),
        name="expert_backward",
    )(og, ids, gates, scales, w, hid, codes)


PARTS = 8


def place_kernel(*refs):
    sources, outputs, buffers, sems = refs[0:4], refs[4:8], refs[8:12], refs[12]

    def views(ref, k):
        if k:
            return [ref]
        return [ref.at[pl.ds(i * (TOK // PARTS), TOK // PARTS)] for i in range(PARTS)]

    pairs = []
    for k in range(4):
        for src, buf, dst in zip(views(sources[k], k), views(buffers[k], k), views(outputs[k], k)):
            i = len(pairs)
            pairs.append(
                (pltpu.make_async_copy(src, buf, sems.at[0, i]), pltpu.make_async_copy(buf, dst, sems.at[1, i]))
            )
    for load, _ in pairs:
        load.start()
    for load, store in pairs:
        load.wait()
        store.start()
    for _, store in pairs:
        store.wait()


def place_call(*arrays):
    hbm = pl.BlockSpec(memory_space=pltpu.HBM)
    return pl.pallas_call(
        place_kernel,
        out_shape=tuple(jax.ShapeDtypeStruct(a.shape, a.dtype) for a in arrays),
        in_specs=[hbm] * 4,
        out_specs=[hbm] * 4,
        scratch_shapes=[pltpu.VMEM(a.shape, a.dtype) for a in arrays]
        + [pltpu.SemaphoreType.DMA((2, PARTS + 3))],
        compiler_params=pltpu.CompilerParams(vmem_limit_bytes=63 * 2**20),
        name="place_outputs",
    )(*arrays)


def local(out_grad, expert_ids, gates, hidden_slots, weights, mom_codes, mom_scales):
    experts = lax.axis_size("expert")
    groups = lax.axis_size("dp")
    tokens_all = out_grad.shape[0] * groups * experts
    ids = expert_ids.T
    factor = math.sqrt(experts / (2.0 * tokens_all))
    results = main_call(
        factor, out_grad, ids, gates.T, mom_scales, weights[0], hidden_slots.reshape(16 * CAP, FF), mom_codes[0]
    )[:4]
    hidden_grad, direction, new_codes, new_scales = place_call(*results)
    return (hidden_grad, direction[None], new_codes[None], new_scales)


def solution(mesh):
    in_specs = (
        P(("dp", "expert"), None),
        P(("dp", "expert"), None),
        P(("dp", "expert"), None),
        P("dp", "expert", None, None, None),
        P("expert", "dp", None),
        P("expert", "dp", None),
        P("expert", "dp"),
    )
    out_specs = (
        P(("dp", "expert"), None, None),
        P("expert", "dp", None),
        P("expert", "dp", None),
        P("expert", "dp"),
    )
    return jax.shard_map(local, mesh=mesh, in_specs=in_specs, out_specs=out_specs, check_vma=False)
```

```python
import functools
import math

import jax
import jax.numpy as jnp
from jax import lax
from jax.experimental import pallas as pl
from jax.experimental.pallas import tpu as pltpu
from jax.sharding import PartitionSpec as P

MESH = pl.DeviceIdType.MESH
bf16 = jnp.bfloat16
f32 = jnp.float32

beta_one = 0.9
beta_two = 0.99
epsilon = 1e-06

D = 2048
FF = 3200
TOK = 256
CAP = 64
HALF = 32
HD = D // 2
ROWS = 80
SHARD = 400
CUT = 208
NCH = 5
C = FF // NCH


def slot_keys(ids):
    tok = ids.shape[1]
    expert = lax.broadcasted_iota(jnp.int32, (16, tok), 0)
    c0 = expert == ids[0:1, :]
    c1 = expert == ids[1:2, :]
    cnt = jnp.where(c0 | c1, 1.0, 0.0).astype(bf16)
    before = jnp.where(
        lax.broadcasted_iota(jnp.int32, (tok, tok), 0) < lax.broadcasted_iota(jnp.int32, (tok, tok), 1), 1.0, 0.0
    ).astype(bf16)
    earlier = jnp.dot(cnt, before, preferred_element_type=f32)
    pos0 = jnp.sum(jnp.where(c0, earlier, 0.0), axis=0, keepdims=True).astype(jnp.int32)
    pos1 = jnp.sum(jnp.where(c1, earlier, 0.0), axis=0, keepdims=True).astype(jnp.int32)
    return ids[0:1, :] * CAP + pos0, ids[1:2, :] * CAP + pos1


def rows_of(start, count):
    return pl.ds(pl.multiple_of(start, 16), count)


def main_kernel(
    og, ids, gates, w, hid,
    hidden_grad,
    ret, pieces, sr, m2a, m2b,
    sa, sb, meta, rr, ww, hv, pb, oo, sums, tt, pk, ost, last,
    ag_s, ag_r, loc, p1_s, p1_r, mt_s, mt_r, p2_s, p2_r, r1_s, r1_r, r2_s, r2_r, rl, sib_s, sib_r, x_s, x_r, tail_s, own_s,
):
    dp = lax.axis_index("dp")
    ex = lax.axis_index("expert")
    x, c = dp // 2, dp % 2
    y, z = ex // 4, ex % 4

    def dev_x(d):
        return (((x + d) % 4) * 2 + c, ex)

    def dev_y(d):
        return (dp, ((y + d) % 4) * 4 + z)

    def dev_z(d):
        return (dp, y * 4 + (z + d) % 4)

    sibling = (x * 2 + 1 - c, ex)

    barrier = pltpu.get_barrier_semaphore()
    peers = [dev_y(1), dev_y(2), dev_y(3), dev_z(1), dev_z(2), dev_z(3), dev_x(1), dev_x(3), sibling]
    for peer in peers:
        pl.semaphore_signal(barrier, inc=1, device_id=peer, device_id_type=MESH)
    pl.semaphore_wait(barrier, len(peers))

    def remote(src, dst, s, r, device):
        return pltpu.make_async_remote_copy(
            src_ref=src, dst_ref=dst, send_sem=s, recv_sem=r, device_id=device, device_id_type=MESH
        )

    def shard_rows(xx, cc, lo, n):
        return rows_of(((xx % 4) * 2 + cc) * SHARD + lo, n)

    H0 = (0, CUT)
    H1 = (CUT, SHARD - CUT)

    def ag_copy(i, xx, cut, device, own):
        lo, n = cut
        there = ww.at[shard_rows(xx, c, lo, n)]
        src = w.at[pl.ds(lo, n)] if own else there
        return remote(src, there, ag_s.at[i], ag_r.at[i], device)

    ag = [
        ag_copy(0, x, H0, dev_x(1), True),
        ag_copy(1, x, H1, dev_x(1), True),
        ag_copy(2, x, H1, dev_x(3), True),
        ag_copy(3, x, H0, dev_x(3), True),
        ag_copy(4, x + 3, H0, dev_x(1), False),
        ag_copy(5, x + 1, H1, dev_x(3), False),
        ag_copy(6, x, (0, SHARD), sibling, True),
        ag_copy(7, x + 3, H0, sibling, False),
        ag_copy(8, x + 3, H1, sibling, False),
        ag_copy(9, x + 1, H1, sibling, False),
        ag_copy(10, x + 1, H0, sibling, False),
        ag_copy(11, x + 2, H0, sibling, False),
        ag_copy(12, x + 2, H1, sibling, False),
    ]
    w_own = pltpu.make_async_copy(w, ww.at[shard_rows(x, c, 0, SHARD)], loc.at[0])
    for i in (0, 2, 1, 3, 6):
        ag[i].start()
    w_own.start()

    h_load = pltpu.make_async_copy(hid, hv, loc.at[8])
    h_load.start()

    def og_copy(i, own_axis, d, half, axis):
        pos = (y, z)[axis]
        src_pos = (pos + (0, 0, 0, 0, 3, 1)[i]) % 4
        rows = half * (TOK // 2)
        there = pb.at[rows_of(src_pos * TOK + rows, TOK // 2), pl.ds(axis * HD, HD)]
        src = og.at[pl.ds(rows, TOK // 2), pl.ds(axis * HD, HD)] if own_axis else there
        k = axis * 6 + i
        return remote(src, there, p1_s.at[k], p1_r.at[k], (dev_y, dev_z)[axis](d))

    def og_copies(axis):
        return [
            og_copy(0, True, 1, 0, axis),
            og_copy(1, True, 1, 1, axis),
            og_copy(2, True, 3, 1, axis),
            og_copy(3, True, 3, 0, axis),
            og_copy(4, False, 1, 0, axis),
            og_copy(5, False, 3, 1, axis),
        ]

    oy, oz = og_copies(0), og_copies(1)
    for i in (0, 2, 1, 3):
        oy[i].start()
        oz[i].start()

    key0, key1 = slot_keys(ids[...])
    for axis, pos in ((0, y), (1, z)):
        meta[axis * 4 + pos, 0:1, :] = key0.astype(f32)
        meta[axis * 4 + pos, 1:2, :] = key1.astype(f32)
        meta[axis * 4 + pos, 2:4, :] = gates[...]
        meta[axis * 4 + pos, 4:8, :] = jnp.zeros((4, TOK), f32)

    def meta_copy(axis, d):
        at = meta.at[axis * 4 + (y, z)[axis]]
        k = axis * 3 + d - 1
        return remote(at, at, mt_s.at[k], mt_r.at[k], (dev_y, dev_z)[axis](d))

    for d in (1, 3, 2):
        meta_copy(0, d).start()
        meta_copy(1, d).start()

    def build(axis, j):
        pos = ((y, z)[axis] + 4 - j) % 4
        info = meta[axis * 4 + pos]
        i = lax.broadcasted_iota(jnp.int32, (4 * CAP, TOK), 0)
        slot = i + y * (4 * CAP) if axis == 0 else (i // CAP) * (4 * CAP) + z * CAP + i % CAP
        slot = slot.astype(f32)
        e0, e1 = slot == info[0:1], slot == info[1:2]
        pick = jnp.where(e0 | e1, 1.0, 0.0).astype(bf16)
        gate = jnp.sum(jnp.where(e0, info[2:3], 0.0) + jnp.where(e1, info[3:4], 0.0), axis=1, keepdims=True)
        cols = pl.ds(axis * HD, HD)
        rows = og[:, cols] if j == 0 else pb[rows_of(pos * TOK, TOK), cols]
        res = jnp.dot(pick, rows, preferred_element_type=f32)
        (sa, sb)[axis][pos] = (res * gate).astype(bf16).reshape(4, CAP, HD)

    A = pl.ds(0, HALF)
    B = pl.ds(HALF, HALF)
    left, right = pl.ds(0, HD), pl.ds(HD, HD)

    def p2a(j, d):
        sy = (y + 4 - j) % 4
        i = j * 3 + d - 1
        return remote(sa.at[sy, (z + d) % 4], rr.at[sy, z, :, left], p2_s.at[i], p2_r.at[i], dev_z(d))

    def p2b(j, d):
        sz = (z + 4 - j) % 4
        i = 12 + j * 3 + d - 1
        return remote(sb.at[sz, (y + d) % 4], rr.at[y, sz, :, right], p2_s.at[i], p2_r.at[i], dev_y(d))

    def p2a_own(j):
        sy = (y + 4 - j) % 4
        return pltpu.make_async_copy(sa.at[sy, z], rr.at[sy, z, :, left], own_s.at[j])

    def p2b_own(j):
        sz = (z + 4 - j) % 4
        return pltpu.make_async_copy(sb.at[sz, y], rr.at[y, sz, :, right], own_s.at[4 + j])

    def dispatch(j):
        build(0, j)
        for d in (1, 3, 2):
            p2a(j, d).start()
        p2a_own(j).start()
        build(1, j)
        for d in (1, 3, 2):
            p2b(j, d).start()
        p2b_own(j).start()

    dispatch(0)

    oy[0].wait_recv()
    oy[4].start()
    oz[0].wait_recv()
    oz[4].start()
    oy[2].wait_recv()
    oy[5].start()
    oz[2].wait_recv()
    oz[5].start()
    for j, i in ((1, 1), (3, 3)):
        oy[i].wait_recv()
        oz[i].wait_recv()
        meta_copy(0, j).wait_recv()
        meta_copy(1, j).wait_recv()
        dispatch(j)

    slot_id = lax.broadcasted_iota(jnp.int32, (16 * CAP, TOK), 0)
    pk[0:TOK, :] = jnp.where(slot_id == key0, 1.0, 0.0).astype(bf16).T
    pk[TOK:, :] = jnp.where(slot_id == key1, 1.0, 0.0).astype(bf16).T

    for i in (4, 5):
        oy[i].wait_recv()
        oz[i].wait_recv()
    meta_copy(0, 2).wait_recv()
    meta_copy(1, 2).wait_recv()
    dispatch(2)

    ag[0].wait_recv()
    ag[4].start()
    ag[7].start()
    ag[2].wait_recv()
    ag[5].start()
    ag[9].start()
    ag[1].wait_recv()
    ag[8].start()
    ag[3].wait_recv()
    ag[10].start()

    w_own.wait()
    for i in range(6, 11):
        ag[i].wait_recv()
    h_load.wait()

    def rows_here(d):
        for k in (1, 3, 2):
            p2a((4 - d) % 4, k).wait_recv()
        p2a_own((4 - d) % 4).wait()
        for j in (0, 1, 3, 2):
            if d:
                p2b(j, 4 - d).wait_recv()
            else:
                p2b_own(j).wait()

    first = ((x + 2) % 4 + 2) % 5

    def chunk(i):
        return (first + i) % NCH

    def product_a(i):
        wj = ww[rows_of(chunk(i) * C, C), :]
        rows = rr[...].reshape(16 * CAP, D)
        res = lax.dot_general(rows, wj, (((1,), (1,)), ((), ())), preferred_element_type=f32)
        oo[i] = res.astype(bf16).reshape(4, 4, CAP, C)

    def product_first(d):
        sy = (y + d) % 4
        wj = ww[rows_of(chunk(0) * C, C), :]
        rows = rr[sy].reshape(4 * CAP, D)
        res = lax.dot_general(rows, wj, (((1,), (1,)), ((), ())), preferred_element_type=f32)
        oo[0, sy] = res.astype(bf16).reshape(4, CAP, C)

    def product_b(i):
        at = chunk(i) * C

        def part(n, carry):
            cols = pl.ds(pl.multiple_of(n * 1024, 1024), 1024)
            hj = hv[:, pl.ds(pl.multiple_of(at, 128), C)]
            rows = rr[:, :, :, cols].reshape(16 * CAP, 1024)
            res = lax.dot_general(hj, rows, (((0,), (0,)), ((), ())), preferred_element_type=f32)
            pb[rows_of(at, C), cols] = res.astype(bf16)
            return carry

        lax.fori_loop(0, D // 1024, part, 0)

    def r1a(j, d):
        return remote(oo.at[j, (y + d) % 4, :, A, :], m2a.at[j, y], r1_s.at[j, d - 1], r1_r.at[j, d - 1], dev_y(d))

    def r1b(j, d):
        return remote(oo.at[j, :, (z + d) % 4, B, :], m2b.at[j, z], r1_s.at[j, 2 + d], r1_r.at[j, 2 + d], dev_z(d))

    def r1a_own(j):
        return pltpu.make_async_copy(oo.at[j, y, :, A, :], m2a.at[j, y], rl.at[j, 0])

    def r1b_own(j):
        return pltpu.make_async_copy(oo.at[j, :, z, B, :], m2b.at[j, z], rl.at[j, 1])

    def back(j):
        return last if j == NCH - 1 else ret.at[chunk(j)]

    def r2a(j, d):
        return remote(
            m2a.at[j, :, (z + d) % 4], back(j).at[:, z, A, :], r2_s.at[j, d - 1], r2_r.at[j, d - 1], dev_z(d)
        )

    def r2b(j, d):
        return remote(
            m2b.at[j, :, (y + d) % 4], back(j).at[y, :, B, :], r2_s.at[j, 2 + d], r2_r.at[j, 2 + d], dev_y(d)
        )

    def r2a_own(j):
        return pltpu.make_async_copy(m2a.at[j, :, z], back(j).at[:, z, A, :], rl.at[j, 2])

    def r2b_own(j):
        return pltpu.make_async_copy(m2b.at[j, :, y], back(j).at[y, :, B, :], rl.at[j, 3])

    def send(j):
        for d in (1, 3, 2):
            r1a(j, d).start()
            r1b(j, d).start()
        r1a_own(j).start()
        r1b_own(j).start()

    def forward(j):
        r1a_own(j).wait()
        for d in (1, 3, 2):
            r1a(j, d).wait_recv()
        for d in (1, 3, 2):
            r2a(j, d).start()
        r2a_own(j).start()
        r1b_own(j).wait()
        for d in (1, 3, 2):
            r1b(j, d).wait_recv()
        for d in (1, 3, 2):
            r2b(j, d).start()
        r2b_own(j).start()

    hop = (2, 1, 3, 0)

    def to_sibling(k):
        return remote(pb.at[shard_rows(x + hop[k], 1 - c, 0, SHARD)], sr.at[k], sib_s.at[k], sib_r.at[k], sibling)

    def add_sibling(k):
        to_sibling(k).wait_recv()
        load = pltpu.make_async_copy(sr.at[k], sums, loc.at[7])
        load.start()
        load.wait()

        def part(i, carry):
            at = shard_rows(x + hop[k], c, i * 80, 80)
            mine = pb[at, :].astype(f32) + sums[rows_of(i * 80, 80), :].astype(f32)
            pb[at, :] = mine.astype(bf16)
            return carry

        lax.fori_loop(0, SHARD // 80, part, 0)

    def far(i):
        lo, n = (H0, H1)[i]
        return remote(
            pb.at[shard_rows(x + 2, c, lo, n)], tt.at[pl.ds(lo, n)], x_s.at[i], x_r.at[i], dev_x((1, 3)[i])
        )

    def add_far(i):
        far(i).wait_recv()
        lo, n = (H0, H1)[i]

        def part(k, carry):
            at = shard_rows(x + (1, 3)[i], c, lo + k * 16, 16)
            mine = pb[at, :].astype(f32) + tt[pl.ds(pl.multiple_of(lo + k * 16, 16), 16), :].astype(f32)
            pb[at, :] = mine.astype(bf16)
            return carry

        lax.fori_loop(0, n // 16, part, 0)

    def near(i, h):
        lo, n = (H0, H1)[h]
        k = 2 + 2 * i + h
        return remote(
            pb.at[shard_rows(x + (1, 3)[i], c, lo, n)],
            pieces.at[i, pl.ds(lo, n)],
            x_s.at[k],
            x_r.at[k],
            dev_x((1, 3)[i]),
        )

    def stage(i):
        buf, at = ((sa, 0), (sb, 0), (rr, 0), (rr, 1), (rr, 2))[i]
        return buf.at[:, :, :, pl.ds(at * C, C)]

    def stage_load(i):
        return pltpu.make_async_copy(ret.at[chunk(i)], stage(i), tail_s.at[i])

    def out_copy(i):
        at = pl.ds(pl.multiple_of(chunk(i) * C, 128), C)
        return pltpu.make_async_copy(ost.at[i % 2], hidden_grad.at[:, :, at], tail_s.at[NCH + i])

    def pick(i):
        r2a_own(i).wait()
        r2b_own(i).wait()
        for d in (1, 3, 2):
            r2a(i, d).wait_recv()
            r2b(i, d).wait_recv()
        if i < NCH - 1:
            stage_load(i).start()
            stage_load(i).wait()
        if i >= 2:
            out_copy(i - 2).wait()
        rows = (last if i == NCH - 1 else stage(i))[...].reshape(16 * CAP, C)
        got = jnp.dot(pk[...], rows, preferred_element_type=f32).astype(bf16)
        ost[i % 2, :, 0, :] = got[0:TOK]
        ost[i % 2, :, 1, :] = got[TOK:]
        out_copy(i).start()

    own_piece = pltpu.make_async_copy(pb.at[shard_rows(x, c, 0, SHARD)], pieces.at[2], tail_s.at[2 * NCH])

    rows_here(0)
    product_first(0)
    r1a_own(0).start()
    for d in (1, 3, 2):
        rows_here(d)
        product_first(d)
        r1a(0, d).start()
    for d in (1, 3, 2):
        r1b(0, d).start()
    r1b_own(0).start()
    for i in range(6):
        oy[i].wait_send()
        oz[i].wait_send()
    product_b(3)
    product_a(1)
    send(1)
    product_b(4)
    to_sibling(0).start()
    forward(0)
    ag[4].wait_recv()
    ag[11].start()
    ag[5].wait_recv()
    ag[12].start()
    product_b(0)
    add_sibling(0)
    far(0).start()
    far(1).start()
    product_a(2)
    send(2)
    forward(1)
    product_b(1)
    product_b(2)
    for k in range(1, 4):
        to_sibling(k).start()
    ag[11].wait_recv()
    ag[12].wait_recv()
    product_a(3)
    send(3)
    add_sibling(1)
    near(0, 1).start()
    add_sibling(2)
    near(1, 0).start()
    forward(2)
    add_far(0)
    near(0, 0).start()
    add_far(1)
    near(1, 1).start()
    product_a(4)
    send(4)
    add_sibling(3)
    own_piece.start()

    for i in range(13):
        ag[i].wait_send()
    for d in (1, 2, 3):
        meta_copy(0, d).wait_send()
        meta_copy(1, d).wait_send()
        for j in range(4):
            p2a(j, d).wait_send()
            p2b(j, d).wait_send()
    pick(0)
    forward(3)
    pick(1)
    forward(4)
    pick(2)
    pick(3)
    pick(4)

    for k in range(4):
        to_sibling(k).wait_send()
    for i in range(2):
        far(i).wait_send()
        for h in range(2):
            near(i, h).wait()
    for j in range(NCH):
        for d in (1, 2, 3):
            r1a(j, d).wait_send()
            r1b(j, d).wait_send()
            r2a(j, d).wait_send()
            r2b(j, d).wait_send()
    own_piece.wait()
    out_copy(3).wait()
    out_copy(4).wait()


def main_call(og, ids, gates, w, hid):
    any_spec = pl.BlockSpec(memory_space=pl.ANY)
    vmem = pl.BlockSpec(memory_space=pltpu.VMEM)
    dma = pltpu.SemaphoreType.DMA
    s = jax.ShapeDtypeStruct
    return pl.pallas_call(
        main_kernel,
        out_shape=(
            s((TOK, 2, FF), bf16),
            s((NCH, 4, 4, CAP, C), bf16),
            s((3, SHARD, D), bf16),
            s((4, SHARD, D), bf16),
            s((NCH, 4, 4, HALF, C), bf16),
            s((NCH, 4, 4, HALF, C), bf16),
        ),
        in_specs=[vmem] * 3 + [any_spec] * 2,
        out_specs=[any_spec] * 6,
        scratch_shapes=[
            pltpu.VMEM((4, 4, CAP, HD), bf16),
            pltpu.VMEM((4, 4, CAP, HD), bf16),
            pltpu.VMEM((8, 8, TOK), f32),
            pltpu.VMEM((4, 4, CAP, D), bf16),
            pltpu.VMEM((FF, D), bf16),
            pltpu.VMEM((16 * CAP, FF), bf16),
            pltpu.VMEM((FF, D), bf16),
            pltpu.VMEM((NCH, 4, 4, CAP, C), bf16),
            pltpu.VMEM((SHARD, D), bf16),
            pltpu.VMEM((SHARD, D), bf16),
            pltpu.VMEM((2 * TOK, 16 * CAP), bf16),
            pltpu.VMEM((2, TOK, 2, C), bf16),
            pltpu.VMEM((4, 4, CAP, C), bf16),
            dma((13,)), dma((13,)), dma((9,)),
            dma((12,)), dma((12,)), dma((6,)), dma((6,)), dma((24,)), dma((24,)),
            dma((NCH, 6)), dma((NCH, 6)), dma((NCH, 6)), dma((NCH, 6)), dma((NCH, 4)),
            dma((4,)), dma((4,)), dma((6,)), dma((6,)), dma((2 * NCH + 5,)), dma((8,)),
        ],
        compiler_params=pltpu.CompilerParams(
            collective_id=0, has_side_effects=True, vmem_limit_bytes=63 * 2**20
        ),
        cost_estimate=pl.CostEstimate(flops=32 * 10**9, bytes_accessed=60 * 10**6, transcendentals=0),
        name="expert_backward",
    )(og, ids, gates, w, hid)


PARTS = 8
STEPS = SHARD // ROWS


def finish_kernel(
    factor, grad, pieces, codes, scales, grad_out, direction, new_codes, new_scales, gbuf, pbuf, cbuf, dbuf, gsem, ssem
):
    def grad_rows(ref, i):
        return ref.at[pl.ds(i * (TOK // PARTS), TOK // PARTS)]

    grad_loads = [
        pltpu.make_async_copy(grad_rows(grad, i), grad_rows(gbuf, i), gsem.at[0, i]) for i in range(PARTS)
    ]
    grad_stores = [
        pltpu.make_async_copy(grad_rows(gbuf, i), grad_rows(grad_out, i), gsem.at[1, i]) for i in range(PARTS)
    ]
    at = [pl.ds(i * ROWS, ROWS) for i in range(STEPS)]
    loads = [
        (
            pltpu.make_async_copy(pieces.at[:, r], pbuf.at[:, r], ssem.at[0, i]),
            pltpu.make_async_copy(codes.at[r], cbuf.at[r], ssem.at[1, i]),
        )
        for i, r in enumerate(at)
    ]
    stores = [
        (
            pltpu.make_async_copy(dbuf.at[r], direction.at[r], ssem.at[2, i]),
            pltpu.make_async_copy(cbuf.at[r], new_codes.at[r], ssem.at[3, i]),
        )
        for i, r in enumerate(at)
    ]
    for pair in loads[:2]:
        for load in pair:
            load.start()
    for load in grad_loads:
        load.start()
    for pair in loads[2:]:
        for load in pair:
            load.start()
    scale_row = scales[...]
    largest_row = jnp.zeros((1, SHARD), f32)
    for i, r in enumerate(at):
        for load in loads[i]:
            load.wait()
        gradient = factor * (pbuf[0, r, :].astype(f32) + pbuf[1, r, :].astype(f32) + pbuf[2, r, :].astype(f32))
        here = lax.broadcasted_iota(jnp.int32, (ROWS, SHARD), 0) + i * ROWS == lax.broadcasted_iota(
            jnp.int32, (ROWS, SHARD), 1
        )
        scale = jnp.sum(jnp.where(here, scale_row, 0.0), axis=1, keepdims=True)
        momentum = cbuf[r, :].astype(f32) * scale
        blended = beta_one * momentum + (1.0 - beta_one) * gradient
        root = lax.rsqrt(jnp.mean(blended * blended, axis=-1, keepdims=True) + epsilon)
        advanced = beta_two * momentum + (1.0 - beta_two) * gradient
        largest = jnp.max(jnp.abs(advanced), axis=-1, keepdims=True) + epsilon
        dbuf[r, :] = jnp.tanh(blended * root).astype(bf16)
        cbuf[r, :] = (advanced * (1.0 / largest)).astype(bf16)
        largest_row += jnp.sum(jnp.where(here, largest, 0.0), axis=0, keepdims=True)
        for store in stores[i]:
            store.start()
        for k in range(2 * i, min(2 * i + 2, PARTS)):
            grad_loads[k].wait()
            grad_stores[k].start()
    new_scales[...] = largest_row
    for pair in stores:
        for store in pair:
            store.wait()
    for store in grad_stores:
        store.wait()


def finish_call(factor, grad, pieces, codes, scales):
    hbm = pl.BlockSpec(memory_space=pltpu.HBM)
    vmem = pl.BlockSpec(memory_space=pltpu.VMEM)
    s = jax.ShapeDtypeStruct
    return pl.pallas_call(
        functools.partial(finish_kernel, factor),
        out_shape=(s(grad.shape, bf16), s((SHARD, D), bf16), s((SHARD, D), bf16), s((1, SHARD), f32)),
        in_specs=[hbm, hbm, hbm, vmem],
        out_specs=[hbm, hbm, hbm, vmem],
        scratch_shapes=[
            pltpu.VMEM(grad.shape, bf16),
            pltpu.VMEM((3, SHARD, D), bf16),
            pltpu.VMEM((SHARD, D), bf16),
            pltpu.VMEM((SHARD, D), bf16),
            pltpu.SemaphoreType.DMA((2, PARTS)),
            pltpu.SemaphoreType.DMA((4, STEPS)),
        ],
        compiler_params=pltpu.CompilerParams(vmem_limit_bytes=63 * 2**20),
        name="step_and_place",
    )(grad, pieces, codes, scales)


def local(out_grad, expert_ids, gates, hidden_slots, weights, mom_codes, mom_scales):
    experts = lax.axis_size("expert")
    groups = lax.axis_size("dp")
    tokens_all = out_grad.shape[0] * groups * experts
    ids = expert_ids.T
    factor = math.sqrt(experts / (2.0 * tokens_all))
    hidden_grad, _, pieces = main_call(
        out_grad, ids, gates.T, weights[0], hidden_slots.reshape(16 * CAP, FF)
    )[:3]
    hidden_grad, direction, new_codes, new_scales = finish_call(
        factor, hidden_grad, pieces, mom_codes[0], mom_scales
    )
    return (hidden_grad, direction[None], new_codes[None], new_scales)


def solution(mesh):
    in_specs = (
        P(("dp", "expert"), None),
        P(("dp", "expert"), None),
        P(("dp", "expert"), None),
        P("dp", "expert", None, None, None),
        P("expert", "dp", None),
        P("expert", "dp", None),
        P("expert", "dp"),
    )
    out_specs = (
        P(("dp", "expert"), None, None),
        P("expert", "dp", None),
        P("expert", "dp", None),
        P("expert", "dp"),
    )
    return jax.shard_map(local, mesh=mesh, in_specs=in_specs, out_specs=out_specs, check_vma=False)
```

```python
import functools
import math

import jax
import jax.numpy as jnp
from jax import lax
from jax.experimental import pallas as pl
from jax.experimental.pallas import tpu as pltpu
from jax.sharding import PartitionSpec as P

MESH = pl.DeviceIdType.MESH
bf16 = jnp.bfloat16
f32 = jnp.float32

beta_one = 0.9
beta_two = 0.99
epsilon = 1e-06

D = 2048
FF = 3200
TOK = 256
CAP = 64
HALF = 32
HD = D // 2
ROWS = 80
SHARD = 400
CUT = 208
NCH = 5
C = FF // NCH


def slot_keys(ids):
    tok = ids.shape[1]
    expert = lax.broadcasted_iota(jnp.int32, (16, tok), 0)
    c0 = expert == ids[0:1, :]
    c1 = expert == ids[1:2, :]
    cnt = jnp.where(c0 | c1, 1.0, 0.0).astype(bf16)
    before = jnp.where(
        lax.broadcasted_iota(jnp.int32, (tok, tok), 0) < lax.broadcasted_iota(jnp.int32, (tok, tok), 1), 1.0, 0.0
    ).astype(bf16)
    earlier = jnp.dot(cnt, before, preferred_element_type=f32)
    pos0 = jnp.sum(jnp.where(c0, earlier, 0.0), axis=0, keepdims=True).astype(jnp.int32)
    pos1 = jnp.sum(jnp.where(c1, earlier, 0.0), axis=0, keepdims=True).astype(jnp.int32)
    return ids[0:1, :] * CAP + pos0, ids[1:2, :] * CAP + pos1


def rows_of(start, count):
    return pl.ds(pl.multiple_of(start, 16), count)


def main_kernel(
    og, ids, gates, w, hid,
    hidden_grad,
    ret, pieces, sr, m2a, m2b,
    sa, sb, meta, rr, ww, hv, pb, oo, sums, tt, pk, ost, last,
    ag_s, ag_r, loc, p1_s, p1_r, mt_s, mt_r, p2_s, p2_r, r1_s, r1_r, r2_s, r2_r, rl, sib_s, sib_r, x_s, x_r, tail_s, own_s,
):
    dp = lax.axis_index("dp")
    ex = lax.axis_index("expert")
    x, c = dp // 2, dp % 2
    y, z = ex // 4, ex % 4

    def dev_x(d):
        return (((x + d) % 4) * 2 + c, ex)

    def dev_y(d):
        return (dp, ((y + d) % 4) * 4 + z)

    def dev_z(d):
        return (dp, y * 4 + (z + d) % 4)

    sibling = (x * 2 + 1 - c, ex)

    barrier = pltpu.get_barrier_semaphore()
    peers = [dev_y(1), dev_y(2), dev_y(3), dev_z(1), dev_z(2), dev_z(3), dev_x(1), dev_x(3), sibling]
    for peer in peers:
        pl.semaphore_signal(barrier, inc=1, device_id=peer, device_id_type=MESH)
    pl.semaphore_wait(barrier, len(peers))

    def remote(src, dst, s, r, device):
        return pltpu.make_async_remote_copy(
            src_ref=src, dst_ref=dst, send_sem=s, recv_sem=r, device_id=device, device_id_type=MESH
        )

    def shard_rows(xx, cc, lo, n):
        return rows_of(((xx % 4) * 2 + cc) * SHARD + lo, n)

    H0 = (0, CUT)
    H1 = (CUT, SHARD - CUT)

    def ag_copy(i, xx, cut, device, own):
        lo, n = cut
        there = ww.at[shard_rows(xx, c, lo, n)]
        src = w.at[pl.ds(lo, n)] if own else there
        return remote(src, there, ag_s.at[i], ag_r.at[i], device)

    ag = [
        ag_copy(0, x, H0, dev_x(1), True),
        ag_copy(1, x, H1, dev_x(1), True),
        ag_copy(2, x, H1, dev_x(3), True),
        ag_copy(3, x, H0, dev_x(3), True),
        ag_copy(4, x + 3, H0, dev_x(1), False),
        ag_copy(5, x + 1, H1, dev_x(3), False),
        ag_copy(6, x, (0, SHARD), sibling, True),
        ag_copy(7, x + 3, H0, sibling, False),
        ag_copy(8, x + 3, H1, sibling, False),
        ag_copy(9, x + 1, H1, sibling, False),
        ag_copy(10, x + 1, H0, sibling, False),
        ag_copy(11, x + 2, H0, sibling, False),
        ag_copy(12, x + 2, H1, sibling, False),
    ]
    w_own = pltpu.make_async_copy(w, ww.at[shard_rows(x, c, 0, SHARD)], loc.at[0])
    for i in (0, 2, 1, 3, 6):
        ag[i].start()
    w_own.start()

    h_load = pltpu.make_async_copy(hid, hv, loc.at[8])
    h_load.start()

    def og_copy(i, own_axis, d, half, axis):
        pos = (y, z)[axis]
        src_pos = (pos + (0, 0, 0, 0, 3, 1)[i]) % 4
        rows = half * (TOK // 2)
        there = pb.at[rows_of(src_pos * TOK + rows, TOK // 2), pl.ds(axis * HD, HD)]
        src = og.at[pl.ds(rows, TOK // 2), pl.ds(axis * HD, HD)] if own_axis else there
        k = axis * 6 + i
        return remote(src, there, p1_s.at[k], p1_r.at[k], (dev_y, dev_z)[axis](d))

    def og_copies(axis):
        return [
            og_copy(0, True, 1, 0, axis),
            og_copy(1, True, 1, 1, axis),
            og_copy(2, True, 3, 1, axis),
            og_copy(3, True, 3, 0, axis),
            og_copy(4, False, 1, 0, axis),
            og_copy(5, False, 3, 1, axis),
        ]

    oy, oz = og_copies(0), og_copies(1)
    for i in (0, 2, 1, 3):
        oy[i].start()
        oz[i].start()

    key0, key1 = slot_keys(ids[...])
    for axis, pos in ((0, y), (1, z)):
        meta[axis * 4 + pos, 0:1, :] = key0.astype(f32)
        meta[axis * 4 + pos, 1:2, :] = key1.astype(f32)
        meta[axis * 4 + pos, 2:4, :] = gates[...]
        meta[axis * 4 + pos, 4:8, :] = jnp.zeros((4, TOK), f32)

    def meta_copy(axis, d):
        at = meta.at[axis * 4 + (y, z)[axis]]
        k = axis * 3 + d - 1
        return remote(at, at, mt_s.at[k], mt_r.at[k], (dev_y, dev_z)[axis](d))

    for d in (1, 3, 2):
        meta_copy(0, d).start()
        meta_copy(1, d).start()

    def build(axis, j):
        pos = ((y, z)[axis] + 4 - j) % 4
        info = meta[axis * 4 + pos]
        i = lax.broadcasted_iota(jnp.int32, (4 * CAP, TOK), 0)
        slot = i + y * (4 * CAP) if axis == 0 else (i // CAP) * (4 * CAP) + z * CAP + i % CAP
        slot = slot.astype(f32)
        e0, e1 = slot == info[0:1], slot == info[1:2]
        pick = jnp.where(e0 | e1, 1.0, 0.0).astype(bf16)
        gate = jnp.sum(jnp.where(e0, info[2:3], 0.0) + jnp.where(e1, info[3:4], 0.0), axis=1, keepdims=True)
        cols = pl.ds(axis * HD, HD)
        rows = og[:, cols] if j == 0 else pb[rows_of(pos * TOK, TOK), cols]
        res = jnp.dot(pick, rows, preferred_element_type=f32)
        (sa, sb)[axis][pos] = (res * gate).astype(bf16).reshape(4, CAP, HD)

    A = pl.ds(0, HALF)
    B = pl.ds(HALF, HALF)
    left, right = pl.ds(0, HD), pl.ds(HD, HD)

    def p2a(j, d):
        sy = (y + 4 - j) % 4
        i = j * 3 + d - 1
        return remote(sa.at[sy, (z + d) % 4], rr.at[sy, z, :, left], p2_s.at[i], p2_r.at[i], dev_z(d))

    def p2b(j, d):
        sz = (z + 4 - j) % 4
        i = 12 + j * 3 + d - 1
        return remote(sb.at[sz, (y + d) % 4], rr.at[y, sz, :, right], p2_s.at[i], p2_r.at[i], dev_y(d))

    def p2a_own(j):
        sy = (y + 4 - j) % 4
        return pltpu.make_async_copy(sa.at[sy, z], rr.at[sy, z, :, left], own_s.at[j])

    def p2b_own(j):
        sz = (z + 4 - j) % 4
        return pltpu.make_async_copy(sb.at[sz, y], rr.at[y, sz, :, right], own_s.at[4 + j])

    def dispatch(j):
        build(0, j)
        for d in (1, 3, 2):
            p2a(j, d).start()
        p2a_own(j).start()
        build(1, j)
        for d in (1, 3, 2):
            p2b(j, d).start()
        p2b_own(j).start()

    dispatch(0)

    oy[0].wait_recv()
    oy[4].start()
    oz[0].wait_recv()
    oz[4].start()
    oy[2].wait_recv()
    oy[5].start()
    oz[2].wait_recv()
    oz[5].start()
    for j, i in ((1, 1), (3, 3)):
        oy[i].wait_recv()
        oz[i].wait_recv()
        meta_copy(0, j).wait_recv()
        meta_copy(1, j).wait_recv()
        dispatch(j)

    slot_id = lax.broadcasted_iota(jnp.int32, (16 * CAP, TOK), 0)
    pk[0:TOK, :] = jnp.where(slot_id == key0, 1.0, 0.0).astype(bf16).T
    pk[TOK:, :] = jnp.where(slot_id == key1, 1.0, 0.0).astype(bf16).T

    for i in (4, 5):
        oy[i].wait_recv()
        oz[i].wait_recv()
    meta_copy(0, 2).wait_recv()
    meta_copy(1, 2).wait_recv()
    dispatch(2)

    ag[0].wait_recv()
    ag[4].start()
    ag[7].start()
    ag[2].wait_recv()
    ag[5].start()
    ag[9].start()
    ag[1].wait_recv()
    ag[8].start()
    ag[3].wait_recv()
    ag[10].start()

    w_own.wait()
    for i in range(6, 11):
        ag[i].wait_recv()
    h_load.wait()

    def rows_here(d):
        for k in (1, 3, 2):
            p2a((4 - d) % 4, k).wait_recv()
        p2a_own((4 - d) % 4).wait()
        for j in (0, 1, 3, 2):
            if d:
                p2b(j, 4 - d).wait_recv()
            else:
                p2b_own(j).wait()

    first = ((x + 2) % 4 + 2) % 5

    def chunk(i):
        return (first + i) % NCH

    def product_a(i):
        wj = ww[rows_of(chunk(i) * C, C), :]
        rows = rr[...].reshape(16 * CAP, D)
        res = lax.dot_general(rows, wj, (((1,), (1,)), ((), ())), preferred_element_type=f32)
        oo[i] = res.astype(bf16).reshape(4, 4, CAP, C)

    def product_first(d):
        sy = (y + d) % 4
        wj = ww[rows_of(chunk(0) * C, C), :]
        rows = rr[sy].reshape(4 * CAP, D)
        res = lax.dot_general(rows, wj, (((1,), (1,)), ((), ())), preferred_element_type=f32)
        oo[0, sy] = res.astype(bf16).reshape(4, CAP, C)

    def product_b(i):
        at = chunk(i) * C

        def part(n, carry):
            cols = pl.ds(pl.multiple_of(n * 1024, 1024), 1024)
            hj = hv[:, pl.ds(pl.multiple_of(at, 128), C)]
            rows = rr[:, :, :, cols].reshape(16 * CAP, 1024)
            res = lax.dot_general(hj, rows, (((0,), (0,)), ((), ())), preferred_element_type=f32)
            pb[rows_of(at, C), cols] = res.astype(bf16)
            return carry

        lax.fori_loop(0, D // 1024, part, 0)

    def r1a(j, d):
        return remote(oo.at[j, (y + d) % 4, :, A, :], m2a.at[j, y], r1_s.at[j, d - 1], r1_r.at[j, d - 1], dev_y(d))

    def r1b(j, d):
        return remote(oo.at[j, :, (z + d) % 4, B, :], m2b.at[j, z], r1_s.at[j, 2 + d], r1_r.at[j, 2 + d], dev_z(d))

    def r1a_own(j):
        return pltpu.make_async_copy(oo.at[j, y, :, A, :], m2a.at[j, y], rl.at[j, 0])

    def r1b_own(j):
        return pltpu.make_async_copy(oo.at[j, :, z, B, :], m2b.at[j, z], rl.at[j, 1])

    def back(j):
        return last if j == NCH - 1 else ret.at[chunk(j)]

    def r2a(j, d):
        return remote(
            m2a.at[j, :, (z + d) % 4], back(j).at[:, z, A, :], r2_s.at[j, d - 1], r2_r.at[j, d - 1], dev_z(d)
        )

    def r2b(j, d):
        return remote(
            m2b.at[j, :, (y + d) % 4], back(j).at[y, :, B, :], r2_s.at[j, 2 + d], r2_r.at[j, 2 + d], dev_y(d)
        )

    def r2a_own(j):
        return pltpu.make_async_copy(m2a.at[j, :, z], back(j).at[:, z, A, :], rl.at[j, 2])

    def r2b_own(j):
        return pltpu.make_async_copy(m2b.at[j, :, y], back(j).at[y, :, B, :], rl.at[j, 3])

    def send(j):
        for d in (1, 3, 2):
            r1a(j, d).start()
            r1b(j, d).start()
        r1a_own(j).start()
        r1b_own(j).start()

    def forward(j):
        r1a_own(j).wait()
        for d in (1, 3, 2):
            r1a(j, d).wait_recv()
        for d in (1, 3, 2):
            r2a(j, d).start()
        r2a_own(j).start()
        r1b_own(j).wait()
        for d in (1, 3, 2):
            r1b(j, d).wait_recv()
        for d in (1, 3, 2):
            r2b(j, d).start()
        r2b_own(j).start()

    hop = (2, 1, 3, 0)

    def to_sibling(k):
        return remote(pb.at[shard_rows(x + hop[k], 1 - c, 0, SHARD)], sr.at[k], sib_s.at[k], sib_r.at[k], sibling)

    def add_sibling(k):
        to_sibling(k).wait_recv()
        load = pltpu.make_async_copy(sr.at[k], sums, loc.at[7])
        load.start()
        load.wait()

        def part(i, carry):
            at = shard_rows(x + hop[k], c, i * 80, 80)
            mine = pb[at, :].astype(f32) + sums[rows_of(i * 80, 80), :].astype(f32)
            pb[at, :] = mine.astype(bf16)
            return carry

        lax.fori_loop(0, SHARD // 80, part, 0)

    def far(i):
        lo, n = (H0, H1)[i]
        return remote(
            pb.at[shard_rows(x + 2, c, lo, n)], tt.at[pl.ds(lo, n)], x_s.at[i], x_r.at[i], dev_x((1, 3)[i])
        )

    def add_far(i):
        far(i).wait_recv()
        lo, n = (H0, H1)[i]

        def part(k, carry):
            at = shard_rows(x + (1, 3)[i], c, lo + k * 16, 16)
            mine = pb[at, :].astype(f32) + tt[pl.ds(pl.multiple_of(lo + k * 16, 16), 16), :].astype(f32)
            pb[at, :] = mine.astype(bf16)
            return carry

        lax.fori_loop(0, n // 16, part, 0)

    def near(i, h):
        lo, n = (H0, H1)[h]
        k = 2 + 2 * i + h
        return remote(
            pb.at[shard_rows(x + (1, 3)[i], c, lo, n)],
            pieces.at[i, pl.ds(lo, n)],
            x_s.at[k],
            x_r.at[k],
            dev_x((1, 3)[i]),
        )

    def stage(i):
        buf, at = ((sa, 0), (sb, 0), (rr, 0), (rr, 1), (rr, 2))[i]
        return buf.at[:, :, :, pl.ds(at * C, C)]

    def stage_load(i):
        return pltpu.make_async_copy(ret.at[chunk(i)], stage(i), tail_s.at[i])

    def out_copy(i):
        at = pl.ds(pl.multiple_of(chunk(i) * C, 128), C)
        return pltpu.make_async_copy(ost.at[i % 2], hidden_grad.at[:, :, at], tail_s.at[NCH + i])

    def pick(i):
        r2a_own(i).wait()
        r2b_own(i).wait()
        for d in (1, 3, 2):
            r2a(i, d).wait_recv()
            r2b(i, d).wait_recv()
        if i < NCH - 1:
            stage_load(i).start()
            stage_load(i).wait()
        if i >= 2:
            out_copy(i - 2).wait()
        rows = (last if i == NCH - 1 else stage(i))[...].reshape(16 * CAP, C)
        got = jnp.dot(pk[...], rows, preferred_element_type=f32).astype(bf16)
        ost[i % 2, :, 0, :] = got[0:TOK]
        ost[i % 2, :, 1, :] = got[TOK:]
        out_copy(i).start()

    own_piece = pltpu.make_async_copy(pb.at[shard_rows(x, c, 0, SHARD)], pieces.at[2], tail_s.at[2 * NCH])

    rows_here(0)
    product_first(0)
    r1a_own(0).start()
    for d in (1, 3, 2):
        rows_here(d)
        product_first(d)
        r1a(0, d).start()
    for d in (1, 3, 2):
        r1b(0, d).start()
    r1b_own(0).start()
    for i in range(6):
        oy[i].wait_send()
        oz[i].wait_send()
    product_b(3)
    product_a(1)
    send(1)
    product_b(4)
    to_sibling(0).start()
    forward(0)
    ag[4].wait_recv()
    ag[11].start()
    ag[5].wait_recv()
    ag[12].start()
    product_b(0)
    add_sibling(0)
    far(0).start()
    far(1).start()
    product_a(2)
    send(2)
    forward(1)
    product_b(1)
    product_b(2)
    for k in range(1, 4):
        to_sibling(k).start()
    ag[11].wait_recv()
    ag[12].wait_recv()
    product_a(3)
    send(3)
    add_sibling(1)
    near(0, 1).start()
    add_sibling(2)
    near(1, 0).start()
    forward(2)
    add_far(0)
    near(0, 0).start()
    add_far(1)
    near(1, 1).start()
    product_a(4)
    send(4)
    add_sibling(3)
    own_piece.start()

    for i in range(13):
        ag[i].wait_send()
    for d in (1, 2, 3):
        meta_copy(0, d).wait_send()
        meta_copy(1, d).wait_send()
        for j in range(4):
            p2a(j, d).wait_send()
            p2b(j, d).wait_send()
    forward(3)
    pick(0)
    pick(1)
    forward(4)
    pick(2)
    pick(3)
    pick(4)

    for k in range(4):
        to_sibling(k).wait_send()
    for i in range(2):
        far(i).wait_send()
        for h in range(2):
            near(i, h).wait()
    for j in range(NCH):
        for d in (1, 2, 3):
            r1a(j, d).wait_send()
            r1b(j, d).wait_send()
            r2a(j, d).wait_send()
            r2b(j, d).wait_send()
    own_piece.wait()
    out_copy(3).wait()
    out_copy(4).wait()


def main_call(og, ids, gates, w, hid):
    any_spec = pl.BlockSpec(memory_space=pl.ANY)
    vmem = pl.BlockSpec(memory_space=pltpu.VMEM)
    dma = pltpu.SemaphoreType.DMA
    s = jax.ShapeDtypeStruct
    return pl.pallas_call(
        main_kernel,
        out_shape=(
            s((TOK, 2, FF), bf16),
            s((NCH, 4, 4, CAP, C), bf16),
            s((3, SHARD, D), bf16),
            s((4, SHARD, D), bf16),
            s((NCH, 4, 4, HALF, C), bf16),
            s((NCH, 4, 4, HALF, C), bf16),
        ),
        in_specs=[vmem] * 3 + [any_spec] * 2,
        out_specs=[any_spec] * 6,
        scratch_shapes=[
            pltpu.VMEM((4, 4, CAP, HD), bf16),
            pltpu.VMEM((4, 4, CAP, HD), bf16),
            pltpu.VMEM((8, 8, TOK), f32),
            pltpu.VMEM((4, 4, CAP, D), bf16),
            pltpu.VMEM((FF, D), bf16),
            pltpu.VMEM((16 * CAP, FF), bf16),
            pltpu.VMEM((FF, D), bf16),
            pltpu.VMEM((NCH, 4, 4, CAP, C), bf16),
            pltpu.VMEM((SHARD, D), bf16),
            pltpu.VMEM((SHARD, D), bf16),
            pltpu.VMEM((2 * TOK, 16 * CAP), bf16),
            pltpu.VMEM((2, TOK, 2, C), bf16),
            pltpu.VMEM((4, 4, CAP, C), bf16),
            dma((13,)), dma((13,)), dma((9,)),
            dma((12,)), dma((12,)), dma((6,)), dma((6,)), dma((24,)), dma((24,)),
            dma((NCH, 6)), dma((NCH, 6)), dma((NCH, 6)), dma((NCH, 6)), dma((NCH, 4)),
            dma((4,)), dma((4,)), dma((6,)), dma((6,)), dma((2 * NCH + 5,)), dma((8,)),
        ],
        compiler_params=pltpu.CompilerParams(
            collective_id=0, has_side_effects=True, vmem_limit_bytes=63 * 2**20
        ),
        cost_estimate=pl.CostEstimate(flops=32 * 10**9, bytes_accessed=60 * 10**6, transcendentals=0),
        name="expert_backward",
    )(og, ids, gates, w, hid)


PARTS = 8
STEPS = SHARD // ROWS


def finish_kernel(
    factor, grad, pieces, codes, scales, grad_out, direction, new_codes, new_scales, gbuf, pbuf, cbuf, dbuf, gsem, ssem
):
    def grad_rows(ref, i):
        return ref.at[pl.ds(i * (TOK // PARTS), TOK // PARTS)]

    grad_loads = [
        pltpu.make_async_copy(grad_rows(grad, i), grad_rows(gbuf, i), gsem.at[0, i]) for i in range(PARTS)
    ]
    grad_stores = [
        pltpu.make_async_copy(grad_rows(gbuf, i), grad_rows(grad_out, i), gsem.at[1, i]) for i in range(PARTS)
    ]
    at = [pl.ds(i * ROWS, ROWS) for i in range(STEPS)]
    loads = [
        (
            pltpu.make_async_copy(pieces.at[:, r], pbuf.at[:, r], ssem.at[0, i]),
            pltpu.make_async_copy(codes.at[r], cbuf.at[r], ssem.at[1, i]),
        )
        for i, r in enumerate(at)
    ]
    stores = [
        (
            pltpu.make_async_copy(dbuf.at[r], direction.at[r], ssem.at[2, i]),
            pltpu.make_async_copy(cbuf.at[r], new_codes.at[r], ssem.at[3, i]),
        )
        for i, r in enumerate(at)
    ]
    for pair in loads:
        for load in pair:
            load.start()
    for load in grad_loads:
        load.start()
    scale_row = scales[...]
    largest_row = jnp.zeros((1, SHARD), f32)
    for i, r in enumerate(at):
        for load in loads[i]:
            load.wait()
        summed = pbuf[0, r, :].astype(f32) + pbuf[1, r, :].astype(f32) + pbuf[2, r, :].astype(f32)
        here = lax.broadcasted_iota(jnp.int32, (ROWS, SHARD), 0) + i * ROWS == lax.broadcasted_iota(
            jnp.int32, (ROWS, SHARD), 1
        )
        scale = jnp.sum(jnp.where(here, scale_row, 0.0), axis=1, keepdims=True)
        coded = cbuf[r, :].astype(f32)
        blended = coded * (beta_one * scale) + ((1.0 - beta_one) * factor) * summed
        root = lax.rsqrt(jnp.mean(blended * blended, axis=-1, keepdims=True) + epsilon)
        advanced = coded * (beta_two * scale) + ((1.0 - beta_two) * factor) * summed
        largest = jnp.max(jnp.abs(advanced), axis=-1, keepdims=True) + epsilon
        dbuf[r, :] = jnp.tanh(blended * root).astype(bf16)
        cbuf[r, :] = (advanced * (1.0 / largest)).astype(bf16)
        largest_row += jnp.sum(jnp.where(here, largest, 0.0), axis=0, keepdims=True)
        for store in stores[i]:
            store.start()
        for k in range(2 * i, min(2 * i + 2, PARTS)):
            grad_loads[k].wait()
            grad_stores[k].start()
    new_scales[...] = largest_row
    for pair in stores:
        for store in pair:
            store.wait()
    for store in grad_stores:
        store.wait()


def finish_call(factor, grad, pieces, codes, scales):
    hbm = pl.BlockSpec(memory_space=pltpu.HBM)
    vmem = pl.BlockSpec(memory_space=pltpu.VMEM)
    s = jax.ShapeDtypeStruct
    return pl.pallas_call(
        functools.partial(finish_kernel, factor),
        out_shape=(s(grad.shape, bf16), s((SHARD, D), bf16), s((SHARD, D), bf16), s((1, SHARD), f32)),
        in_specs=[hbm, hbm, hbm, vmem],
        out_specs=[hbm, hbm, hbm, vmem],
        scratch_shapes=[
            pltpu.VMEM(grad.shape, bf16),
            pltpu.VMEM((3, SHARD, D), bf16),
            pltpu.VMEM((SHARD, D), bf16),
            pltpu.VMEM((SHARD, D), bf16),
            pltpu.SemaphoreType.DMA((2, PARTS)),
            pltpu.SemaphoreType.DMA((4, STEPS)),
        ],
        compiler_params=pltpu.CompilerParams(vmem_limit_bytes=63 * 2**20),
        name="step_and_place",
    )(grad, pieces, codes, scales)


def local(out_grad, expert_ids, gates, hidden_slots, weights, mom_codes, mom_scales):
    experts = lax.axis_size("expert")
    groups = lax.axis_size("dp")
    tokens_all = out_grad.shape[0] * groups * experts
    ids = expert_ids.T
    factor = math.sqrt(experts / (2.0 * tokens_all))
    hidden_grad, _, pieces = main_call(
        out_grad, ids, gates.T, weights[0], hidden_slots.reshape(16 * CAP, FF)
    )[:3]
    hidden_grad, direction, new_codes, new_scales = finish_call(
        factor, hidden_grad, pieces, mom_codes[0], mom_scales
    )
    return (hidden_grad, direction[None], new_codes[None], new_scales)


def solution(mesh):
    in_specs = (
        P(("dp", "expert"), None),
        P(("dp", "expert"), None),
        P(("dp", "expert"), None),
        P("dp", "expert", None, None, None),
        P("expert", "dp", None),
        P("expert", "dp", None),
        P("expert", "dp"),
    )
    out_specs = (
        P(("dp", "expert"), None, None),
        P("expert", "dp", None),
        P("expert", "dp", None),
        P("expert", "dp"),
    )
    return jax.shard_map(local, mesh=mesh, in_specs=in_specs, out_specs=out_specs, check_vma=False)
```
